32 devices in a mesh: dp: 8 (over y, x, core), mp: 4 (over z).
Axes of the slice: x: 2, y: 2, z: 4, core: 2. Of those that a mesh axis runs over, the one named last changes fastest.
Arguments:
- inputs: bfloat16 [16384, 1024], P('mp', 'dp'), may hold values from -6 to 6
- cotangent: bfloat16 [16384, 1024], P('mp', 'dp'), may hold values from -6 to 6
- r_factor: bfloat16 [1, 128, 128, 128], P(None, 'mp'), may hold values from -0.5 to 0.5
- l_factor: bfloat16 [1, 128, 128, 128], P(None, 'mp'), may hold values from -0.5 to 0.5
Outputs:
- outputs: bfloat16 [16384, 1024], P('mp', 'dp')
- grad_inputs: bfloat16 [16384, 1024], P('mp', 'dp')
- grad_r: float32 [1, 128, 128, 128], P(None, 'mp', 'dp')
- grad_l: float32 [1, 128, 128, 128], P(None, 'mp', 'dp')
The draws below stay inside these ranges and needn't reach their ends.
All inputs are finite; a program needn't handle non-finite values.
Results may differ from the reference program's by a relative error of at most 0.0063.
Values may be sent and summed in bfloat16 or wider, within the bound.
A program may use at most 64 MiB of HBM per device.

```python
import jax
import jax.numpy as jnp
from jax import lax

BLK = 128
WIDTH = 16384
LAYERS = 1
TOK_DEV = 128
TOKENS = 1024


def block_levels(rng, shape, cuts, smallest, largest):
    gain, own = 1.0, jax.random.fold_in(rng, 6)
    for position, blocks in cuts:
        draws = jnp.exp(jax.random.uniform(jax.random.fold_in(own, position), (blocks,), jnp.float32, smallest / len(cuts), largest / len(cuts)))
        gain = gain * jnp.repeat(draws, shape[position] // blocks).reshape([-1 if axis == position else 1 for axis in range(len(shape))])
    return gain


def centred(own_key, extent, deviation, reach, split=(), dtype=jnp.bfloat16):
    drawn = jax.random.normal(own_key, extent, jnp.float32) * deviation
    if len(split) > 0:
        drawn = block_levels(own_key, extent, split, -0.22, 0.18) * drawn
    return jnp.clip(drawn, min=-reach, max=reach).astype(dtype)


def setup_inputs(seed: int = 0) -> dict:
    splits = jax.random.split(jax.random.key(seed), 5)
    inputs = centred(splits[0], (WIDTH, TOKENS), 1.0, 6.0, ((0, 4), (1, 8)))
    cotangent = centred(splits[1], (WIDTH, TOKENS), 1.0, 6.0, ((0, 4), (1, 8)))
    r_factor = centred(splits[2], (LAYERS, BLK, BLK, BLK), BLK ** -0.5, 0.5, ((1, 4),))
    l_factor = centred(splits[3], (LAYERS, BLK, BLK, BLK), BLK ** -0.5, 0.5, ((1, 4),))
    return dict(inputs=inputs, cotangent=cotangent, r_factor=r_factor, l_factor=l_factor)


def activate(values):
    return jax.nn.gelu(values, approximate=True)

def reference(inputs, cotangent, r_factor, l_factor):
    count = TOKENS // TOK_DEV
    f32 = jnp.float32
    bf16 = jnp.bfloat16
    inputs_b = inputs.reshape(BLK, BLK, count, TOK_DEV).transpose(2, 0, 1, 3)
    cotan_b = cotangent.reshape(BLK, BLK, count, TOK_DEV).transpose(2, 0, 1, 3)
    rights = r_factor.astype(f32)
    lefts = l_factor.astype(f32)

    def block_step(totals, piece_pair):
        sum_r, sum_l = totals
        current, grad_now = piece_pair
        saved = []
        for layer_index in range(LAYERS):
            first_out = jnp.einsum('ikt,ikj->ijt', current.astype(f32), rights[layer_index]).astype(bf16)
            pre_act = jnp.einsum('ijt,jim->jmt', first_out.astype(f32), lefts[layer_index])
            saved.append((current, first_out, pre_act))
            current = activate(pre_act).astype(bf16)
        result = current
        for layer_index in reversed(range(LAYERS)):
            layer_in, first_out, pre_act = saved[layer_index]
            back_fn = jax.vjp(activate, pre_act)[1]
            grad_pre = back_fn(grad_now.astype(f32))[0].astype(bf16)
            sum_l = sum_l.at[layer_index].add(jnp.einsum('ijt,jmt->jim', first_out.astype(f32), grad_pre.astype(f32)))
            grad_first = jnp.einsum('jmt,jim->ijt', grad_pre.astype(f32), lefts[layer_index]).astype(bf16)
            sum_r = sum_r.at[layer_index].add(jnp.einsum('ikt,ijt->ikj', layer_in.astype(f32), grad_first.astype(f32)))
            grad_now = jnp.einsum('ijt,ikj->ikt', grad_first.astype(f32), rights[layer_index]).astype(bf16)
        return ((sum_r, sum_l), (result, grad_now))
    zeros = jnp.zeros((LAYERS, BLK, BLK, BLK), f32)
    (sum_r, sum_l), (results, grads) = lax.scan(block_step, (zeros, zeros), (inputs_b, cotan_b))
    scale = float(TOKENS) ** (-0.5)
    outputs = results.transpose(1, 2, 0, 3).reshape(WIDTH, TOKENS)
    grad_inputs = grads.transpose(1, 2, 0, 3).reshape(WIDTH, TOKENS)
    return (outputs, grad_inputs, sum_r * scale, sum_l * scale)
```

```python
import functools

import jax
import jax.numpy as jnp
from jax import lax
from jax.experimental import pallas as pl
from jax.experimental.pallas import tpu as pltpu
from jax.sharding import PartitionSpec as P

MESH = pl.DeviceIdType.MESH
F32 = jnp.float32
BF16 = jnp.bfloat16


def dot(left, right, left_dim, right_dim):
    return lax.dot_general(
        left, right, (((left_dim,), (right_dim,)), ((), ())), preferred_element_type=F32
    )


def gelu_and_slope(v):
    c0, c1 = 0.7978845608028654, 0.044715
    square = v * v
    tanh = jnp.tanh(c0 * v * (1.0 + c1 * square))
    half = 0.5 + 0.5 * tanh
    slope = half + 0.5 * v * (1.0 - tanh * tanh) * (c0 + (3.0 * c0 * c1) * square)
    return v * half, slope


def remote(src, dst, send_sem, recv_sem, axis, target):
    return pltpu.make_async_remote_copy(
        src_ref=src,
        dst_ref=dst,
        send_sem=send_sem,
        recv_sem=recv_sem,
        device_id={axis: target},
        device_id_type=MESH,
    )


def kernel(
    cfg,
    a_hbm, g_hbm, r_hbm, l_hbm,
    out_hbm, gi_hbm, gr_hbm, gl_hbm,
    a_v, g_v, r_v, l_v,
    fo32, fs, fr,
    gf32, gs, gb,
    out_v, gi_v,
    tl_s, tl_r, tr_s, tr_r,
    gl_v, gr_v,
    in_sem, out_sem,
    fs_sem, fr_sem, gs_sem, gb_sem,
    ls_sem, lr_sem, rs_sem, rr_sem,
):
    M, D, nb, B, T, rows, scale, NC, H, G = cfg
    jc, hj, ic = nb // NC, nb // H, nb // G
    mp, dp = lax.axis_index("mp"), lax.axis_index("dp")

    loads = [
        pltpu.make_async_copy(src, dst, in_sem.at[n])
        for n, (src, dst) in enumerate(
            ((a_hbm, a_v), (r_hbm, r_v), (l_hbm, l_v), (g_hbm, g_v))
        )
    ]
    for load in loads:
        load.start()

    barrier = pltpu.get_barrier_semaphore()
    for s in range(1, M):
        pl.semaphore_signal(
            barrier, inc=1, device_id={"mp": lax.rem(mp + s, M)}, device_id_type=MESH
        )
    for s in range(1, D):
        pl.semaphore_signal(
            barrier, inc=1, device_id={"dp": lax.rem(dp + s, D)}, device_id_type=MESH
        )

    loads[0].wait()
    loads[1].wait()

    def first(i, carry):
        fo32[pl.ds(i, B, stride=nb), :] = dot(r_v[i], a_v[i], 0, 0)
        return carry

    lax.fori_loop(0, nb, first, 0, unroll=4)
    pl.semaphore_wait(barrier, (M - 1) + (D - 1))

    mine = pl.multiple_of(mp * nb, nb)
    forward = []
    for c in range(NC):
        step = []
        for s in range(1, M):
            target = lax.rem(mp + s, M)
            base = target * nb + c * jc

            def pack(j, carry, base=base):
                at = pl.multiple_of((base + j) * nb, nb)
                fs[base + j] = fo32[pl.ds(at, nb), :].astype(BF16)
                return carry

            lax.fori_loop(0, jc, pack, 0, unroll=4)
            copy = remote(
                fs.at[pl.ds(base, jc)],
                fr.at[pl.ds(c * jc, jc), pl.ds(mine, nb)],
                fs_sem.at[c, s - 1],
                fr_sem.at[c, s - 1],
                "mp",
                target,
            )
            copy.start()
            step.append(copy)
        forward.append(step)

    def own(j, carry):
        at = pl.multiple_of((mine + j) * nb, nb)
        fr[j, pl.ds(mine, nb), :] = fo32[pl.ds(at, nb), :].astype(BF16)
        return carry

    lax.fori_loop(0, nb, own, 0, unroll=4)
    loads[2].wait()
    loads[3].wait()

    def second(jj, carry):
        x, left = fr[jj], l_v[jj]
        value, slope = gelu_and_slope(dot(left, x, 0, 0))
        out_v[jj] = value.astype(BF16)
        grad_pre = (g_v[jj].astype(F32) * slope).astype(BF16)
        gf32[pl.ds(pl.multiple_of(jj * B, B), B), :] = dot(left, grad_pre, 1, 0)
        term = (dot(x, grad_pre, 1, 1) * scale).astype(BF16)
        for d in range(D):
            tl_s[d, jj] = term[d * rows : (d + 1) * rows]
        return carry

    back, sums_l = [], []
    per_half = NC // H
    for h in range(H):
        for c in range(h * per_half, (h + 1) * per_half):
            for copy in forward[c]:
                copy.wait_recv()
            lax.fori_loop(c * jc, (c + 1) * jc, second, 0, unroll=2)

        at_j = pl.multiple_of(mine + h * hj, hj)
        for g in range(G):
            for s in range(1, M):
                target = lax.rem(mp + s, M)
                base = target * nb + g * ic

                def turn(i, carry, base=base):
                    part = gf32[pl.ds(h * hj * B + base + i, hj, stride=B), :]
                    gs[base + i, pl.ds(h * hj, hj), :] = part.astype(BF16)
                    return carry

                lax.fori_loop(0, ic, turn, 0, unroll=4)
                copy = remote(
                    gs.at[pl.ds(base, ic), pl.ds(h * hj, hj)],
                    gb.at[pl.ds(g * ic, ic), pl.ds(at_j, hj)],
                    gs_sem.at[h * G + g, s - 1],
                    gb_sem.at[h * G + g, s - 1],
                    "mp",
                    target,
                )
                copy.start()
                back.append((g, copy))

        def turn_own(i, carry):
            part = gf32[pl.ds(h * hj * B + mine + i, hj, stride=B), :]
            gb[i, pl.ds(at_j, hj), :] = part.astype(BF16)
            return carry

        lax.fori_loop(0, nb, turn_own, 0, unroll=4)
        for s in range(1, D):
            target = lax.rem(dp + s, D)
            copy = remote(
                tl_s.at[target, pl.ds(h * hj, hj)],
                tl_r.at[s - 1, pl.ds(h * hj, hj)],
                ls_sem.at[h, s - 1],
                lr_sem.at[h, s - 1],
                "dp",
                target,
            )
            copy.start()
            sums_l.append(copy)

    stores = [pltpu.make_async_copy(out_v, out_hbm, out_sem.at[0])]
    stores[0].start()

    def add_l(jj, carry):
        total = tl_s[dp, jj].astype(F32)
        for s in range(D - 1):
            total = total + tl_r[s, jj].astype(F32)
        gl_v[jj] = total
        return carry

    for copy in sums_l:
        copy.wait_recv()
    lax.fori_loop(0, nb, add_l, 0, unroll=2)
    stores.append(pltpu.make_async_copy(gl_v, gl_hbm, out_sem.at[1]))
    stores[-1].start()

    def last(ii, carry):
        y = gb[ii]
        gi_v[ii] = dot(r_v[ii], y, 1, 0).astype(BF16)
        term = (dot(a_v[ii], y, 1, 1) * scale).astype(BF16)
        for d in range(D):
            tr_s[d, ii] = term[d * rows : (d + 1) * rows]
        return carry

    sums_r = []
    for g in range(G):
        for group, copy in back:
            if group == g:
                copy.wait_recv()
        lax.fori_loop(g * ic, (g + 1) * ic, last, 0, unroll=2)
        step = []
        for s in range(1, D):
            target = lax.rem(dp + s, D)
            copy = remote(
                tr_s.at[target, pl.ds(g * ic, ic)],
                tr_r.at[s - 1, pl.ds(g * ic, ic)],
                rs_sem.at[g, s - 1],
                rr_sem.at[g, s - 1],
                "dp",
                target,
            )
            copy.start()
            step.append(copy)
        sums_r.append(step)
    stores.append(pltpu.make_async_copy(gi_v, gi_hbm, out_sem.at[2]))
    stores[-1].start()

    def add_r(ii, carry):
        total = tr_s[dp, ii].astype(F32)
        for s in range(D - 1):
            total = total + tr_r[s, ii].astype(F32)
        gr_v[ii] = total
        return carry

    for g in range(G):
        for copy in sums_r[g]:
            copy.wait_recv()
        lax.fori_loop(g * ic, (g + 1) * ic, add_r, 0, unroll=2)
    stores.append(pltpu.make_async_copy(gr_v, gr_hbm, out_sem.at[3]))
    stores[-1].start()

    for step in forward + sums_r:
        for copy in step:
            copy.wait_send()
    for _, copy in back:
        copy.wait_send()
    for copy in sums_l:
        copy.wait_send()
    for store in stores:
        store.wait()


def fused(M, D, inputs, cotangent, r_factor, l_factor):
    nb, B = r_factor.shape[1], r_factor.shape[2]
    T = inputs.shape[1]
    rows = B // D
    scale = float(D * T) ** (-0.5)
    NC, H, G = 4, 2, 4
    cfg = (M, D, nb, B, T, rows, scale, NC, H, G)
    sem = pltpu.SemaphoreType.DMA
    flops = 6 * 2 * nb * B * B * T
    outputs, grad_inputs, grad_r, grad_l = pl.pallas_call(
        functools.partial(kernel, cfg),
        out_shape=(
            jax.ShapeDtypeStruct((nb, B, T), BF16),
            jax.ShapeDtypeStruct((nb, B, T), BF16),
            jax.ShapeDtypeStruct((nb, rows, B), F32),
            jax.ShapeDtypeStruct((nb, rows, B), F32),
        ),
        in_specs=[pl.BlockSpec(memory_space=pl.ANY)] * 4,
        out_specs=[pl.BlockSpec(memory_space=pl.ANY)] * 4,
        scratch_shapes=[
            pltpu.VMEM((nb, B, T), BF16),
            pltpu.VMEM((nb, B, T), BF16),
            pltpu.VMEM((nb, B, B), BF16),
            pltpu.VMEM((nb, B, B), BF16),
            pltpu.VMEM((B * nb, T), F32),
            pltpu.VMEM((B, nb, T), BF16),
            pltpu.VMEM((nb, B, T), BF16),
            pltpu.VMEM((nb * B, T), F32),
            pltpu.VMEM((B, nb, T), BF16),
            pltpu.VMEM((nb, B, T), BF16),
            pltpu.VMEM((nb, B, T), BF16),
            pltpu.VMEM((nb, B, T), BF16),
            pltpu.VMEM((D, nb, rows, B), BF16),
            pltpu.VMEM((D - 1, nb, rows, B), BF16),
            pltpu.VMEM((D, nb, rows, B), BF16),
            pltpu.VMEM((D - 1, nb, rows, B), BF16),
            pltpu.VMEM((nb, rows, B), F32),
            pltpu.VMEM((nb, rows, B), F32),
            sem((4,)),
            sem((4,)),
            sem((NC, M - 1)),
            sem((NC, M - 1)),
            sem((H * G, M - 1)),
            sem((H * G, M - 1)),
            sem((H, D - 1)),
            sem((H, D - 1)),
            sem((G, D - 1)),
            sem((G, D - 1)),
        ],
        compiler_params=pltpu.CompilerParams(
            collective_id=0, has_side_effects=True, vmem_limit_bytes=48 * 2**20
        ),
        cost_estimate=pl.CostEstimate(
            flops=flops, bytes_accessed=8 * nb * B * T * 2, transcendentals=nb * B * T
        ),
        name="monarch",
    )(
        inputs.reshape(nb, B, T),
        cotangent.reshape(nb, B, T),
        r_factor[0],
        l_factor[0],
    )
    return (
        outputs.reshape(nb * B, T),
        grad_inputs.reshape(nb * B, T),
        grad_r[None],
        grad_l[None],
    )


def plain(M, D, inputs, cotangent, r_factor, l_factor):
    nb, B = r_factor.shape[1], r_factor.shape[2]
    T = inputs.shape[1]
    scale = float(D * T) ** (-0.5)
    right, left = r_factor[0], l_factor[0]
    current = inputs.reshape(nb, B, T)
    first_out = jnp.einsum("ikt,ikj->ijt", current, right, preferred_element_type=F32)
    received = lax.all_to_all(
        first_out.astype(BF16), "mp", split_axis=1, concat_axis=0, tiled=True
    )
    pre_act = jnp.einsum("ijt,jim->jmt", received, left, preferred_element_type=F32)
    value, slope = gelu_and_slope(pre_act)
    grad_pre = (cotangent.reshape(nb, B, T).astype(F32) * slope).astype(BF16)
    term_l = jnp.einsum("ijt,jmt->jim", received, grad_pre, preferred_element_type=F32)
    grad_l = lax.psum_scatter(term_l * scale, "dp", scatter_dimension=1, tiled=True)
    grad_first = jnp.einsum("jmt,jim->ijt", grad_pre, left, preferred_element_type=F32)
    returned = lax.all_to_all(
        grad_first.astype(BF16), "mp", split_axis=0, concat_axis=1, tiled=True
    )
    spread = jnp.einsum("ijt,ikj->ikt", returned, right, preferred_element_type=F32)
    term_r = jnp.einsum("ikt,ijt->ikj", current, returned, preferred_element_type=F32)
    grad_r = lax.psum_scatter(term_r * scale, "dp", scatter_dimension=1, tiled=True)
    return (
        value.astype(BF16).reshape(nb * B, T),
        spread.astype(BF16).reshape(nb * B, T),
        grad_r[None],
        grad_l[None],
    )


def solution(mesh):
    M, D = mesh.shape["mp"], mesh.shape["dp"]

    def shards(inputs, cotangent, r_factor, l_factor):
        nb, B = r_factor.shape[1], r_factor.shape[2]
        tiled = nb % 32 == 0 and (B // D) % 16 == 0 and M > 1 and D > 1
        return (fused if tiled else plain)(M, D, inputs, cotangent, r_factor, l_factor)

    return jax.shard_map(
        shards,
        mesh=mesh,
        in_specs=(P("mp", "dp"), P("mp", "dp"), P(None, "mp"), P(None, "mp")),
        out_specs=(P("mp", "dp"), P("mp", "dp"), P(None, "mp", "dp"), P(None, "mp", "dp")),
        check_vma=False,
    )
```

```python
import functools

import jax
import jax.numpy as jnp
from jax import lax
from jax.experimental import pallas as pl
from jax.experimental.pallas import tpu as pltpu
from jax.sharding import PartitionSpec as P

MESH = pl.DeviceIdType.MESH
F32 = jnp.float32
BF16 = jnp.bfloat16
AHEAD = 2


def dot(left, right, left_dim, right_dim):
    return lax.dot_general(
        left, right, (((left_dim,), (right_dim,)), ((), ())), preferred_element_type=F32
    )


def gelu_and_slope(v):
    c0, c1 = 0.7978845608028654, 0.044715
    square = v * v
    tanh = jnp.tanh(c0 * v * (1.0 + c1 * square))
    half = 0.5 + 0.5 * tanh
    slope = half + 0.5 * v * (1.0 - tanh * tanh) * (c0 + (3.0 * c0 * c1) * square)
    return v * half, slope


def remote(src, dst, send_sem, recv_sem, axis, target):
    return pltpu.make_async_remote_copy(
        src_ref=src,
        dst_ref=dst,
        send_sem=send_sem,
        recv_sem=recv_sem,
        device_id={axis: target},
        device_id_type=MESH,
    )


def kernel(
    cfg,
    a_hbm, g_hbm, r_hbm, l_hbm,
    out_hbm, gi_hbm, gr_hbm, gl_hbm,
    a_v, g_v, r_v, l_v,
    fo32, fs, fr,
    gf32, gs, gb,
    out_v, gi_v,
    tl_s, tl_r, tr_s, tr_r,
    gl_v, gr_v,
    in_sem, out_sem,
    fs_sem, fr_sem, gs_sem, gb_sem,
    ls_sem, lr_sem, rs_sem, rr_sem,
):
    M, D, nb, B, T, rows, scale, NC, H, G = cfg
    jc, hj, ic = nb // NC, nb // H, nb // G
    mp, dp = lax.axis_index("mp"), lax.axis_index("dp")

    half = nb // 2
    loads = []
    for src, dst, parts in (
        (a_hbm, a_v, 2), (r_hbm, r_v, 2), (l_hbm, l_v, 1), (g_hbm, g_v, 1)
    ):
        for p in range(parts):
            at = pl.ds(p * (nb // parts), nb // parts)
            loads.append(
                pltpu.make_async_copy(src.at[at], dst.at[at], in_sem.at[len(loads)])
            )
    for n in (0, 2, 1, 3, 4, 5):
        loads[n].start()

    barrier = pltpu.get_barrier_semaphore()
    for s in range(1, M):
        pl.semaphore_signal(
            barrier, inc=1, device_id={"mp": lax.rem(mp + s, M)}, device_id_type=MESH
        )
    for s in range(1, D):
        pl.semaphore_signal(
            barrier, inc=1, device_id={"dp": lax.rem(dp + s, D)}, device_id_type=MESH
        )

    def first(i, carry):
        fo32[pl.ds(i, B, stride=nb), :] = dot(r_v[i], a_v[i], 0, 0)
        return carry

    mine = pl.multiple_of(mp * nb, nb)
    forward = [[] for _ in range(NC)]
    for p in range(2):
        loads[p].wait()
        loads[2 + p].wait()
        lax.fori_loop(p * half, (p + 1) * half, first, 0, unroll=4)
        if p == 0:
            pl.semaphore_wait(barrier, (M - 1) + (D - 1))
        for c in range(NC):
            for s in range(1, M):
                target = lax.rem(mp + s, M)
                base = target * nb + c * jc

                def pack(j, carry, base=base, p=p):
                    at = pl.multiple_of((base + j) * nb + p * half, half)
                    fs[base + j, pl.ds(p * half, half), :] = fo32[pl.ds(at, half), :].astype(BF16)
                    return carry

                lax.fori_loop(0, jc, pack, 0, unroll=4)
                copy = remote(
                    fs.at[pl.ds(base, jc), pl.ds(p * half, half)],
                    fr.at[pl.ds(c * jc, jc), pl.ds(pl.multiple_of(mine + p * half, half), half)],
                    fs_sem.at[c * 2 + p, s - 1],
                    fr_sem.at[c * 2 + p, s - 1],
                    "mp",
                    target,
                )
                copy.start()
                forward[c].append(copy)

    def own(j, carry):
        at = pl.multiple_of((mine + j) * nb, nb)
        fr[j, pl.ds(mine, nb), :] = fo32[pl.ds(at, nb), :].astype(BF16)
        return carry

    lax.fori_loop(0, nb, own, 0, unroll=4)
    loads[4].wait()
    loads[5].wait()

    def second(jj, carry):
        x, left = fr[jj], l_v[jj]
        value, slope = gelu_and_slope(dot(left, x, 0, 0))
        out_v[jj] = value.astype(BF16)
        grad_pre = (g_v[jj].astype(F32) * slope).astype(BF16)
        gf32[pl.ds(pl.multiple_of(jj * B, B), B), :] = dot(left, grad_pre, 1, 0)
        term = (dot(x, grad_pre, 1, 1) * scale).astype(BF16)
        for d in range(D):
            tl_s[d, jj] = term[d * rows : (d + 1) * rows]
        return carry

    back, sums_l = [[] for _ in range(G)], []

    def turn(h, g, s):
        base = lax.rem(mp + s, M) * nb + g * ic

        def one(i, carry):
            part = gf32[pl.ds(h * hj * B + base + i, hj, stride=B), :]
            gs[base + i, pl.ds(h * hj, hj), :] = part.astype(BF16)
            return carry

        lax.fori_loop(0, ic, one, 0, unroll=4)

    def turn_own(h):
        at_j = pl.multiple_of(mine + h * hj, hj)

        def one(i, carry):
            part = gf32[pl.ds(h * hj * B + mine + i, hj, stride=B), :]
            gb[i, pl.ds(at_j, hj), :] = part.astype(BF16)
            return carry

        lax.fori_loop(0, nb, one, 0, unroll=4)

    def send_back(h, g, s):
        target = lax.rem(mp + s, M)
        base = target * nb + g * ic
        at_j = pl.multiple_of(mine + h * hj, hj)
        copy = remote(
            gs.at[pl.ds(base, ic), pl.ds(h * hj, hj)],
            gb.at[pl.ds(g * ic, ic), pl.ds(at_j, hj)],
            gs_sem.at[h * G + g, s - 1],
            gb_sem.at[h * G + g, s - 1],
            "mp",
            target,
        )
        copy.start()
        back[g].append(copy)

    def turn_and_send(h, g):
        for s in range(1, M):
            turn(h, g, s)
            send_back(h, g, s)

    def send_l(h):
        for s in range(1, D):
            target = lax.rem(dp + s, D)
            copy = remote(
                tl_s.at[target, pl.ds(h * hj, hj)],
                tl_r.at[s - 1, pl.ds(h * hj, hj)],
                ls_sem.at[h, s - 1],
                lr_sem.at[h, s - 1],
                "dp",
                target,
            )
            copy.start()
            sums_l.append(copy)

    for c in range(NC):
        for copy in forward[c]:
            copy.wait_recv()
        lax.fori_loop(c * jc, (c + 1) * jc, second, 0, unroll=2)
        if c == 1:
            send_l(0)
            turn_own(0)
        if c == 2:
            for g in range(G):
                turn_and_send(0, g)
    for g in range(AHEAD):
        turn_and_send(1, g)
    send_l(1)
    turn_own(1)

    stores = [pltpu.make_async_copy(out_v, out_hbm, out_sem.at[0])]
    stores[0].start()

    def add_l(jj, carry):
        total = tl_s[dp, jj].astype(F32)
        for s in range(D - 1):
            total = total + tl_r[s, jj].astype(F32)
        gl_v[jj] = total
        return carry

    def last(ii, carry):
        y = gb[ii]
        gi_v[ii] = dot(r_v[ii], y, 1, 0).astype(BF16)
        term = (dot(a_v[ii], y, 1, 1) * scale).astype(BF16)
        for d in range(D):
            tr_s[d, ii] = term[d * rows : (d + 1) * rows]
        return carry

    sums_r = []
    for g in range(G):
        for copy in back[g]:
            copy.wait_recv()
        if g + AHEAD < G:
            turn_and_send(1, g + AHEAD)
        lax.fori_loop(g * ic, (g + 1) * ic, last, 0, unroll=2)
        step = []
        for s in range(1, D):
            target = lax.rem(dp + s, D)
            copy = remote(
                tr_s.at[target, pl.ds(g * ic, ic)],
                tr_r.at[s - 1, pl.ds(g * ic, ic)],
                rs_sem.at[g, s - 1],
                rr_sem.at[g, s - 1],
                "dp",
                target,
            )
            copy.start()
            step.append(copy)
        sums_r.append(step)
        if g == G - 3:
            for copy in sums_l:
                copy.wait_recv()
            lax.fori_loop(0, nb, add_l, 0, unroll=2)
            stores.append(pltpu.make_async_copy(gl_v, gl_hbm, out_sem.at[1]))
            stores[-1].start()
    stores.append(pltpu.make_async_copy(gi_v, gi_hbm, out_sem.at[2]))
    stores[-1].start()

    def add_r(ii, carry):
        total = tr_s[dp, ii].astype(F32)
        for s in range(D - 1):
            total = total + tr_r[s, ii].astype(F32)
        gr_v[ii] = total
        return carry

    for g in range(G):
        for copy in sums_r[g]:
            copy.wait_recv()
        lax.fori_loop(g * ic, (g + 1) * ic, add_r, 0, unroll=2)
    stores.append(pltpu.make_async_copy(gr_v, gr_hbm, out_sem.at[3]))
    stores[-1].start()

    for step in forward + back + sums_r:
        for copy in step:
            copy.wait_send()
    for copy in sums_l:
        copy.wait_send()
    for store in stores:
        store.wait()


def write_out(*refs):
    done = refs[8]
    copies = [pltpu.make_async_copy(refs[n], refs[4 + n], done.at[n]) for n in range(4)]
    for copy in copies:
        copy.start()
    for copy in copies:
        copy.wait()


def fused(M, D, inputs, cotangent, r_factor, l_factor):
    nb, B = r_factor.shape[1], r_factor.shape[2]
    T = inputs.shape[1]
    rows = B // D
    scale = float(D * T) ** (-0.5)
    NC, H, G = 4, 2, 4
    cfg = (M, D, nb, B, T, rows, scale, NC, H, G)
    sem = pltpu.SemaphoreType.DMA
    flops = 6 * 2 * nb * B * B * T
    results = pl.pallas_call(
        functools.partial(kernel, cfg),
        out_shape=(
            jax.ShapeDtypeStruct((nb, B, T), BF16),
            jax.ShapeDtypeStruct((nb, B, T), BF16),
            jax.ShapeDtypeStruct((nb, rows, B), F32),
            jax.ShapeDtypeStruct((nb, rows, B), F32),
        ),
        in_specs=[pl.BlockSpec(memory_space=pltpu.HBM)] * 4,
        out_specs=[pl.BlockSpec(memory_space=pl.ANY)] * 4,
        scratch_shapes=[
            pltpu.VMEM((nb, B, T), BF16),
            pltpu.VMEM((nb, B, T), BF16),
            pltpu.VMEM((nb, B, B), BF16),
            pltpu.VMEM((nb, B, B), BF16),
            pltpu.VMEM((B * nb, T), F32),
            pltpu.VMEM((B, nb, T), BF16),
            pltpu.VMEM((nb, B, T), BF16),
            pltpu.VMEM((nb * B, T), F32),
            pltpu.VMEM((B, nb, T), BF16),
            pltpu.VMEM((nb, B, T), BF16),
            pltpu.VMEM((nb, B, T), BF16),
            pltpu.VMEM((nb, B, T), BF16),
            pltpu.VMEM((D, nb, rows, B), BF16),
            pltpu.VMEM((D - 1, nb, rows, B), BF16),
            pltpu.VMEM((D, nb, rows, B), BF16),
            pltpu.VMEM((D - 1, nb, rows, B), BF16),
            pltpu.VMEM((nb, rows, B), F32),
            pltpu.VMEM((nb, rows, B), F32),
            sem((6,)),
            sem((4,)),
            sem((NC * 2, M - 1)),
            sem((NC * 2, M - 1)),
            sem((H * G, M - 1)),
            sem((H * G, M - 1)),
            sem((H, D - 1)),
            sem((H, D - 1)),
            sem((G, D - 1)),
            sem((G, D - 1)),
        ],
        compiler_params=pltpu.CompilerParams(
            collective_id=0, has_side_effects=True, vmem_limit_bytes=62 * 2**20
        ),
        cost_estimate=pl.CostEstimate(
            flops=flops, bytes_accessed=8 * nb * B * T * 2, transcendentals=nb * B * T
        ),
        name="monarch",
    )(
        inputs.reshape(nb, B, T),
        cotangent.reshape(nb, B, T),
        r_factor[0],
        l_factor[0],
    )
    outputs, grad_inputs, grad_r, grad_l = pl.pallas_call(
        write_out,
        out_shape=[jax.ShapeDtypeStruct(x.shape, x.dtype) for x in results],
        in_specs=[pl.BlockSpec(memory_space=pl.ANY)] * 4,
        out_specs=[pl.BlockSpec(memory_space=pltpu.HBM)] * 4,
        scratch_shapes=[sem((4,))],
        name="write_out",
    )(*results)
    return (
        outputs.reshape(nb * B, T),
        grad_inputs.reshape(nb * B, T),
        grad_r[None],
        grad_l[None],
    )


def plain(M, D, inputs, cotangent, r_factor, l_factor):
    nb, B = r_factor.shape[1], r_factor.shape[2]
    T = inputs.shape[1]
    scale = float(D * T) ** (-0.5)
    right, left = r_factor[0], l_factor[0]
    current = inputs.reshape(nb, B, T)
    first_out = jnp.einsum("ikt,ikj->ijt", current, right, preferred_element_type=F32)
    received = lax.all_to_all(
        first_out.astype(BF16), "mp", split_axis=1, concat_axis=0, tiled=True
    )
    pre_act = jnp.einsum("ijt,jim->jmt", received, left, preferred_element_type=F32)
    value, slope = gelu_and_slope(pre_act)
    grad_pre = (cotangent.reshape(nb, B, T).astype(F32) * slope).astype(BF16)
    term_l = jnp.einsum("ijt,jmt->jim", received, grad_pre, preferred_element_type=F32)
    grad_l = lax.psum_scatter(term_l * scale, "dp", scatter_dimension=1, tiled=True)
    grad_first = jnp.einsum("jmt,jim->ijt", grad_pre, left, preferred_element_type=F32)
    returned = lax.all_to_all(
        grad_first.astype(BF16), "mp", split_axis=0, concat_axis=1, tiled=True
    )
    spread = jnp.einsum("ijt,ikj->ikt", returned, right, preferred_element_type=F32)
    term_r = jnp.einsum("ikt,ijt->ikj", current, returned, preferred_element_type=F32)
    grad_r = lax.psum_scatter(term_r * scale, "dp", scatter_dimension=1, tiled=True)
    return (
        value.astype(BF16).reshape(nb * B, T),
        spread.astype(BF16).reshape(nb * B, T),
        grad_r[None],
        grad_l[None],
    )


def solution(mesh):
    M, D = mesh.shape["mp"], mesh.shape["dp"]

    def shards(inputs, cotangent, r_factor, l_factor):
        nb, B = r_factor.shape[1], r_factor.shape[2]
        tiled = nb % 32 == 0 and (B // D) % 16 == 0 and M > 1 and D > 1
        return (fused if tiled else plain)(M, D, inputs, cotangent, r_factor, l_factor)

    return jax.shard_map(
        shards,
        mesh=mesh,
        in_specs=(P("mp", "dp"), P("mp", "dp"), P(None, "mp"), P(None, "mp")),
        out_specs=(P("mp", "dp"), P("mp", "dp"), P(None, "mp", "dp"), P(None, "mp", "dp")),
        check_vma=False,
    )
```

```python
import functools

import jax
import jax.numpy as jnp
from jax import lax
from jax.experimental import pallas as pl
from jax.experimental.pallas import tpu as pltpu
from jax.sharding import PartitionSpec as P

MESH = pl.DeviceIdType.MESH
F32 = jnp.float32
BF16 = jnp.bfloat16
AHEAD = 2


def dot(left, right, left_dim, right_dim):
    return lax.dot_general(
        left, right, (((left_dim,), (right_dim,)), ((), ())), preferred_element_type=F32
    )


def gelu_and_slope(v):
    c0, c1 = 0.7978845608028654, 0.044715
    square = v * v
    tanh = jnp.tanh(c0 * v * (1.0 + c1 * square))
    half = 0.5 + 0.5 * tanh
    slope = half + 0.5 * v * (1.0 - tanh * tanh) * (c0 + (3.0 * c0 * c1) * square)
    return v * half, slope


def remote(src, dst, send_sem, recv_sem, axis, target):
    return pltpu.make_async_remote_copy(
        src_ref=src,
        dst_ref=dst,
        send_sem=send_sem,
        recv_sem=recv_sem,
        device_id={axis: target},
        device_id_type=MESH,
    )


def kernel(
    cfg,
    a_hbm, g_hbm, r_hbm, l_hbm,
    out_hbm, gi_hbm, gr_hbm, gl_hbm,
    a_v, g_v, r_v, l_v,
    fo32, fs, fr,
    gf32, gs, gb,
    out_v, gi_v,
    tl_s, tl_r, tr_s, tr_r,
    gl_v, gr_v,
    in_sem, out_sem,
    fs_sem, fr_sem, gs_sem, gb_sem,
    ls_sem, lr_sem, rs_sem, rr_sem,
):
    M, D, nb, B, T, rows, scale, NC, H, G = cfg
    jc, hj, ic = nb // NC, nb // H, nb // G
    mp, dp = lax.axis_index("mp"), lax.axis_index("dp")

    half = nb // 2
    loads = []
    for src, dst, parts in (
        (a_hbm, a_v, 2), (r_hbm, r_v, 2), (l_hbm, l_v, 1), (g_hbm, g_v, 1)
    ):
        for p in range(parts):
            at = pl.ds(p * (nb // parts), nb // parts)
            loads.append(
                pltpu.make_async_copy(src.at[at], dst.at[at], in_sem.at[len(loads)])
            )
    for n in (0, 2, 1, 3, 4, 5):
        loads[n].start()

    barrier = pltpu.get_barrier_semaphore()
    for s in range(1, M):
        pl.semaphore_signal(
            barrier, inc=1, device_id={"mp": lax.rem(mp + s, M)}, device_id_type=MESH
        )
    for s in range(1, D):
        pl.semaphore_signal(
            barrier, inc=1, device_id={"dp": lax.rem(dp + s, D)}, device_id_type=MESH
        )

    def first(i, carry):
        fo32[pl.ds(i, B, stride=nb), :] = dot(r_v[i], a_v[i], 0, 0)
        return carry

    mine = pl.multiple_of(mp * nb, nb)
    forward = [[] for _ in range(NC)]
    def send_forward(c, start, size):
        for s in range(1, M):
            target = lax.rem(mp + s, M)
            base = target * nb + c * jc

            def pack(j, carry, base=base):
                at = pl.multiple_of((base + j) * nb + start, half)
                fs[base + j, pl.ds(start, size), :] = fo32[pl.ds(at, size), :].astype(BF16)
                return carry

            lax.fori_loop(0, jc, pack, 0, unroll=4)
            slot = c * 2 + start // half
            copy = remote(
                fs.at[pl.ds(base, jc), pl.ds(start, size)],
                fr.at[pl.ds(c * jc, jc), pl.ds(pl.multiple_of(mine + start, half), size)],
                fs_sem.at[slot, s - 1],
                fr_sem.at[slot, s - 1],
                "mp",
                target,
            )
            copy.start()
            forward[c].append(copy)

    for p in range(2):
        loads[p].wait()
        loads[2 + p].wait()
        lax.fori_loop(p * half, (p + 1) * half, first, 0, unroll=4)
        if p == 0:
            pl.semaphore_wait(barrier, (M - 1) + (D - 1))
        for c in range(AHEAD):
            send_forward(c, p * half, half)

    def own(j, carry):
        at = pl.multiple_of((mine + j) * nb, nb)
        fr[j, pl.ds(mine, nb), :] = fo32[pl.ds(at, nb), :].astype(BF16)
        return carry

    lax.fori_loop(0, nb, own, 0, unroll=4)
    loads[4].wait()
    loads[5].wait()

    def second(jj, carry):
        x, left = fr[jj], l_v[jj]
        value, slope = gelu_and_slope(dot(left, x, 0, 0))
        out_v[jj] = value.astype(BF16)
        grad_pre = (g_v[jj].astype(F32) * slope).astype(BF16)
        gf32[pl.ds(pl.multiple_of(jj * B, B), B), :] = dot(left, grad_pre, 1, 0)
        term = (dot(x, grad_pre, 1, 1) * scale).astype(BF16)
        for d in range(D):
            tl_s[d, jj] = term[d * rows : (d + 1) * rows]
        return carry

    back, sums_l = [[] for _ in range(G)], []

    def turn(h, g, s):
        base = lax.rem(mp + s, M) * nb + g * ic

        def one(i, carry):
            part = gf32[pl.ds(h * hj * B + base + i, hj, stride=B), :]
            gs[base + i, pl.ds(h * hj, hj), :] = part.astype(BF16)
            return carry

        lax.fori_loop(0, ic, one, 0, unroll=4)

    def turn_own(h):
        at_j = pl.multiple_of(mine + h * hj, hj)

        def one(i, carry):
            part = gf32[pl.ds(h * hj * B + mine + i, hj, stride=B), :]
            gb[i, pl.ds(at_j, hj), :] = part.astype(BF16)
            return carry

        lax.fori_loop(0, nb, one, 0, unroll=4)

    def send_back(h, g, s):
        target = lax.rem(mp + s, M)
        base = target * nb + g * ic
        at_j = pl.multiple_of(mine + h * hj, hj)
        copy = remote(
            gs.at[pl.ds(base, ic), pl.ds(h * hj, hj)],
            gb.at[pl.ds(g * ic, ic), pl.ds(at_j, hj)],
            gs_sem.at[h * G + g, s - 1],
            gb_sem.at[h * G + g, s - 1],
            "mp",
            target,
        )
        copy.start()
        back[g].append(copy)

    def turn_and_send(h, g):
        for s in range(1, M):
            turn(h, g, s)
            send_back(h, g, s)

    def send_l(h):
        for s in range(1, D):
            target = lax.rem(dp + s, D)
            copy = remote(
                tl_s.at[target, pl.ds(h * hj, hj)],
                tl_r.at[s - 1, pl.ds(h * hj, hj)],
                ls_sem.at[h, s - 1],
                lr_sem.at[h, s - 1],
                "dp",
                target,
            )
            copy.start()
            sums_l.append(copy)

    for c in range(NC):
        for copy in forward[c]:
            copy.wait_recv()
        if c + AHEAD < NC:
            send_forward(c + AHEAD, 0, nb)
        else:
            first_group = (c + AHEAD - NC) * (G // AHEAD)
            for g in range(first_group, first_group + G // AHEAD):
                turn_and_send(0, g)
        lax.fori_loop(c * jc, (c + 1) * jc, second, 0, unroll=2)
        if c == 1:
            send_l(0)
            turn_own(0)
    for g in range(AHEAD):
        turn_and_send(1, g)
    send_l(1)
    turn_own(1)

    stores = [pltpu.make_async_copy(out_v, out_hbm, out_sem.at[0])]
    stores[0].start()

    def add_l(jj, carry):
        total = tl_s[dp, jj].astype(F32)
        for s in range(D - 1):
            total = total + tl_r[s, jj].astype(F32)
        gl_v[jj] = total
        return carry

    def last(ii, carry):
        y = gb[ii]
        gi_v[ii] = dot(r_v[ii], y, 1, 0).astype(BF16)
        term = (dot(a_v[ii], y, 1, 1) * scale).astype(BF16)
        for d in range(D):
            tr_s[d, ii] = term[d * rows : (d + 1) * rows]
        return carry

    sums_r = []
    for g in range(G):
        for copy in back[g]:
            copy.wait_recv()
        if g + AHEAD < G:
            turn_and_send(1, g + AHEAD)
        lax.fori_loop(g * ic, (g + 1) * ic, last, 0, unroll=2)
        step = []
        for s in range(1, D):
            target = lax.rem(dp + s, D)
            copy = remote(
                tr_s.at[target, pl.ds(g * ic, ic)],
                tr_r.at[s - 1, pl.ds(g * ic, ic)],
                rs_sem.at[g, s - 1],
                rr_sem.at[g, s - 1],
                "dp",
                target,
            )
            copy.start()
            step.append(copy)
        sums_r.append(step)
        if g == G - 3:
            for copy in sums_l:
                copy.wait_recv()
            lax.fori_loop(0, nb, add_l, 0, unroll=2)
            stores.append(pltpu.make_async_copy(gl_v, gl_hbm, out_sem.at[1]))
            stores[-1].start()
    stores.append(pltpu.make_async_copy(gi_v, gi_hbm, out_sem.at[2]))
    stores[-1].start()

    def add_r(ii, carry):
        total = tr_s[dp, ii].astype(F32)
        for s in range(D - 1):
            total = total + tr_r[s, ii].astype(F32)
        gr_v[ii] = total
        return carry

    for g in range(G):
        for copy in sums_r[g]:
            copy.wait_recv()
        lax.fori_loop(g * ic, (g + 1) * ic, add_r, 0, unroll=2)
    stores.append(pltpu.make_async_copy(gr_v, gr_hbm, out_sem.at[3]))
    stores[-1].start()

    for step in forward + back + sums_r:
        for copy in step:
            copy.wait_send()
    for copy in sums_l:
        copy.wait_send()
    for store in stores:
        store.wait()


def write_out(*refs):
    sources, results, held, (in_sem, out_sem) = refs[:4], refs[4:8], refs[8:12], refs[12:]
    pieces = []
    for src, mid, dst, parts in zip(sources, held, results, (2, 2, 1, 1)):
        size = src.shape[0] // parts
        for p in range(parts):
            at = pl.ds(p * size, size)
            n = len(pieces)
            pieces.append((
                pltpu.make_async_copy(src.at[at], mid.at[at], in_sem.at[n]),
                pltpu.make_async_copy(mid.at[at], dst.at[at], out_sem.at[n]),
            ))
    for load, _ in pieces:
        load.start()
    for load, store in pieces:
        load.wait()
        store.start()
    for _, store in pieces:
        store.wait()


def fused(M, D, inputs, cotangent, r_factor, l_factor):
    nb, B = r_factor.shape[1], r_factor.shape[2]
    T = inputs.shape[1]
    rows = B // D
    scale = float(D * T) ** (-0.5)
    NC, H, G = 4, 2, 4
    cfg = (M, D, nb, B, T, rows, scale, NC, H, G)
    sem = pltpu.SemaphoreType.DMA
    flops = 6 * 2 * nb * B * B * T
    results = pl.pallas_call(
        functools.partial(kernel, cfg),
        out_shape=(
            jax.ShapeDtypeStruct((nb, B, T), BF16),
            jax.ShapeDtypeStruct((nb, B, T), BF16),
            jax.ShapeDtypeStruct((nb, rows, B), F32),
            jax.ShapeDtypeStruct((nb, rows, B), F32),
        ),
        in_specs=[pl.BlockSpec(memory_space=pltpu.HBM)] * 4,
        out_specs=[pl.BlockSpec(memory_space=pl.ANY)] * 4,
        scratch_shapes=[
            pltpu.VMEM((nb, B, T), BF16),
            pltpu.VMEM((nb, B, T), BF16),
            pltpu.VMEM((nb, B, B), BF16),
            pltpu.VMEM((nb, B, B), BF16),
            pltpu.VMEM((B * nb, T), F32),
            pltpu.VMEM((B, nb, T), BF16),
            pltpu.VMEM((nb, B, T), BF16),
            pltpu.VMEM((nb * B, T), F32),
            pltpu.VMEM((B, nb, T), BF16),
            pltpu.VMEM((nb, B, T), BF16),
            pltpu.VMEM((nb, B, T), BF16),
            pltpu.VMEM((nb, B, T), BF16),
            pltpu.VMEM((D, nb, rows, B), BF16),
            pltpu.VMEM((D - 1, nb, rows, B), BF16),
            pltpu.VMEM((D, nb, rows, B), BF16),
            pltpu.VMEM((D - 1, nb, rows, B), BF16),
            pltpu.VMEM((nb, rows, B), F32),
            pltpu.VMEM((nb, rows, B), F32),
            sem((6,)),
            sem((4,)),
            sem((NC * 2, M - 1)),
            sem((NC * 2, M - 1)),
            sem((H * G, M - 1)),
            sem((H * G, M - 1)),
            sem((H, D - 1)),
            sem((H, D - 1)),
            sem((G, D - 1)),
            sem((G, D - 1)),
        ],
        compiler_params=pltpu.CompilerParams(
            collective_id=0, has_side_effects=True, vmem_limit_bytes=62 * 2**20
        ),
        cost_estimate=pl.CostEstimate(
            flops=flops, bytes_accessed=8 * nb * B * T * 2, transcendentals=nb * B * T
        ),
        name="monarch",
    )(
        inputs.reshape(nb, B, T),
        cotangent.reshape(nb, B, T),
        r_factor[0],
        l_factor[0],
    )
    outputs, grad_inputs, grad_r, grad_l = pl.pallas_call(
        write_out,
        out_shape=[jax.ShapeDtypeStruct(x.shape, x.dtype) for x in results],
        in_specs=[pl.BlockSpec(memory_space=pl.ANY)] * 4,
        out_specs=[pl.BlockSpec(memory_space=pltpu.HBM)] * 4,
        scratch_shapes=[pltpu.VMEM(x.shape, x.dtype) for x in results] + [sem((6,)), sem((6,))],
        compiler_params=pltpu.CompilerParams(vmem_limit_bytes=62 * 2**20),
        name="write_out",
    )(*results)
    return (
        outputs.reshape(nb * B, T),
        grad_inputs.reshape(nb * B, T),
        grad_r[None],
        grad_l[None],
    )


def plain(M, D, inputs, cotangent, r_factor, l_factor):
    nb, B = r_factor.shape[1], r_factor.shape[2]
    T = inputs.shape[1]
    scale = float(D * T) ** (-0.5)
    right, left = r_factor[0], l_factor[0]
    current = inputs.reshape(nb, B, T)
    first_out = jnp.einsum("ikt,ikj->ijt", current, right, preferred_element_type=F32)
    received = lax.all_to_all(
        first_out.astype(BF16), "mp", split_axis=1, concat_axis=0, tiled=True
    )
    pre_act = jnp.einsum("ijt,jim->jmt", received, left, preferred_element_type=F32)
    value, slope = gelu_and_slope(pre_act)
    grad_pre = (cotangent.reshape(nb, B, T).astype(F32) * slope).astype(BF16)
    term_l = jnp.einsum("ijt,jmt->jim", received, grad_pre, preferred_element_type=F32)
    grad_l = lax.psum_scatter(term_l * scale, "dp", scatter_dimension=1, tiled=True)
    grad_first = jnp.einsum("jmt,jim->ijt", grad_pre, left, preferred_element_type=F32)
    returned = lax.all_to_all(
        grad_first.astype(BF16), "mp", split_axis=0, concat_axis=1, tiled=True
    )
    spread = jnp.einsum("ijt,ikj->ikt", returned, right, preferred_element_type=F32)
    term_r = jnp.einsum("ikt,ijt->ikj", current, returned, preferred_element_type=F32)
    grad_r = lax.psum_scatter(term_r * scale, "dp", scatter_dimension=1, tiled=True)
    return (
        value.astype(BF16).reshape(nb * B, T),
        spread.astype(BF16).reshape(nb * B, T),
        grad_r[None],
        grad_l[None],
    )


def solution(mesh):
    M, D = mesh.shape["mp"], mesh.shape["dp"]

    def shards(inputs, cotangent, r_factor, l_factor):
        nb, B = r_factor.shape[1], r_factor.shape[2]
        tiled = nb % 32 == 0 and (B // D) % 16 == 0 and M > 1 and D > 1
        return (fused if tiled else plain)(M, D, inputs, cotangent, r_factor, l_factor)

    return jax.shard_map(
        shards,
        mesh=mesh,
        in_specs=(P("mp", "dp"), P("mp", "dp"), P(None, "mp"), P(None, "mp")),
        out_specs=(P("mp", "dp"), P("mp", "dp"), P(None, "mp", "dp"), P(None, "mp", "dp")),
        check_vma=False,
    )
```

```python
import functools

import jax
import jax.numpy as jnp
from jax import lax
from jax.experimental import pallas as pl
from jax.experimental.pallas import tpu as pltpu
from jax.sharding import PartitionSpec as P

MESH = pl.DeviceIdType.MESH
F32 = jnp.float32
BF16 = jnp.bfloat16
AHEAD = 2


def dot(left, right, left_dim, right_dim):
    return lax.dot_general(
        left, right, (((left_dim,), (right_dim,)), ((), ())), preferred_element_type=F32
    )


def gelu_and_slope(v):
    c0, c1 = 0.7978845608028654, 0.044715
    square = v * v
    tanh = jnp.tanh(c0 * v * (1.0 + c1 * square))
    half = 0.5 + 0.5 * tanh
    slope = half + 0.5 * v * (1.0 - tanh * tanh) * (c0 + (3.0 * c0 * c1) * square)
    return v * half, slope


def remote(src, dst, send_sem, recv_sem, axis, target):
    return pltpu.make_async_remote_copy(
        src_ref=src,
        dst_ref=dst,
        send_sem=send_sem,
        recv_sem=recv_sem,
        device_id={axis: target},
        device_id_type=MESH,
    )


def kernel(
    cfg,
    a_hbm, g_hbm, r_hbm, l_hbm,
    out_hbm, gi_hbm, gr_hbm, gl_hbm,
    a_v, g_v, r_v, l_v,
    fo32, fs, fr,
    gf32, gs, gb,
    out_v, gi_v,
    tl_s, tl_r, tr_s, tr_p, tr_c, tr_r,
    gl_v, gr_v,
    in_sem, out_sem,
    fs_sem, fr_sem, gs_sem, gb_sem,
    ls_sem, lr_sem, ps_sem, pr_sem, rs_sem, rr_sem,
):
    M, D, nb, B, T, rows, scale, NC, H, GROUPS = cfg
    jc, hj = nb // NC, nb // H
    mp, dp = lax.axis_index("mp"), lax.axis_index("dp")

    half = nb // 2
    loads = []
    for src, dst, parts in (
        (a_hbm, a_v, 2), (r_hbm, r_v, 2), (l_hbm, l_v, 1), (g_hbm, g_v, 1)
    ):
        for p in range(parts):
            at = pl.ds(p * (nb // parts), nb // parts)
            loads.append(
                pltpu.make_async_copy(src.at[at], dst.at[at], in_sem.at[len(loads)])
            )
    for n in (0, 2, 1, 3, 4, 5):
        loads[n].start()

    barrier = pltpu.get_barrier_semaphore()
    for s in range(1, M):
        pl.semaphore_signal(
            barrier, inc=1, device_id={"mp": lax.rem(mp + s, M)}, device_id_type=MESH
        )
    for s in range(1, D):
        pl.semaphore_signal(
            barrier, inc=1, device_id={"dp": lax.rem(dp + s, D)}, device_id_type=MESH
        )

    def first(i, carry):
        fo32[pl.ds(i, B, stride=nb), :] = dot(r_v[i], a_v[i], 0, 0)
        return carry

    mine = pl.multiple_of(mp * nb, nb)
    forward = [[] for _ in range(NC)]
    def send_forward(c, start, size):
        for s in range(1, M):
            target = lax.rem(mp + s, M)
            base = target * nb + c * jc

            def pack(j, carry, base=base):
                at = pl.multiple_of((base + j) * nb + start, half)
                fs[base + j, pl.ds(start, size), :] = fo32[pl.ds(at, size), :].astype(BF16)
                return carry

            lax.fori_loop(0, jc, pack, 0, unroll=4)
            slot = c * 2 + start // half
            copy = remote(
                fs.at[pl.ds(base, jc), pl.ds(start, size)],
                fr.at[pl.ds(c * jc, jc), pl.ds(pl.multiple_of(mine + start, half), size)],
                fs_sem.at[slot, s - 1],
                fr_sem.at[slot, s - 1],
                "mp",
                target,
            )
            copy.start()
            forward[c].append(copy)

    for p in range(2):
        loads[p].wait()
        loads[2 + p].wait()
        lax.fori_loop(p * half, (p + 1) * half, first, 0, unroll=4)
        if p == 0:
            pl.semaphore_wait(barrier, (M - 1) + (D - 1))
        for c in range(AHEAD):
            send_forward(c, p * half, half)

    def own(j, carry):
        at = pl.multiple_of((mine + j) * nb, nb)
        fr[j, pl.ds(mine, nb), :] = fo32[pl.ds(at, nb), :].astype(BF16)
        return carry

    lax.fori_loop(0, nb, own, 0, unroll=4)
    loads[4].wait()
    loads[5].wait()

    def second(jj, carry):
        x, left = fr[jj], l_v[jj]
        value, slope = gelu_and_slope(dot(left, x, 0, 0))
        out_v[jj] = value.astype(BF16)
        grad_pre = (g_v[jj].astype(F32) * slope).astype(BF16)
        gf32[pl.ds(pl.multiple_of(jj * B, B), B), :] = dot(left, grad_pre, 1, 0)
        term = (dot(x, grad_pre, 1, 1) * scale).astype(BF16)
        for d in range(D):
            tl_s[d, jj] = term[d * rows : (d + 1) * rows]
        return carry

    back, sums_l = [[] for _ in range(len(GROUPS))], []

    def turn(h, start, size, s):
        base = lax.rem(mp + s, M) * nb + start

        def one(i, carry):
            part = gf32[pl.ds(h * hj * B + base + i, hj, stride=B), :]
            gs[base + i, pl.ds(h * hj, hj), :] = part.astype(BF16)
            return carry

        lax.fori_loop(0, size, one, 0, unroll=4)

    def turn_own(h):
        at_j = pl.multiple_of(mine + h * hj, hj)

        def one(i, carry):
            part = gf32[pl.ds(h * hj * B + mine + i, hj, stride=B), :]
            gb[i, pl.ds(at_j, hj), :] = part.astype(BF16)
            return carry

        lax.fori_loop(0, nb, one, 0, unroll=4)

    def turn_and_send(n):
        h, start, size = GROUPS[n]
        for s in range(1, M):
            turn(h, start, size, s)
            target = lax.rem(mp + s, M)
            at_j = pl.multiple_of(mine + h * hj, hj)
            copy = remote(
                gs.at[pl.ds(target * nb + start, size), pl.ds(h * hj, hj)],
                gb.at[pl.ds(start, size), pl.ds(at_j, hj)],
                gs_sem.at[n, s - 1],
                gb_sem.at[n, s - 1],
                "mp",
                target,
            )
            copy.start()
            back[n].append(copy)

    def send_l(h):
        for s in range(1, D):
            target = lax.rem(dp + s, D)
            copy = remote(
                tl_s.at[target, pl.ds(h * hj, hj)],
                tl_r.at[s - 1, pl.ds(h * hj, hj)],
                ls_sem.at[h, s - 1],
                lr_sem.at[h, s - 1],
                "dp",
                target,
            )
            copy.start()
            sums_l.append(copy)

    for c in range(NC):
        for copy in forward[c]:
            copy.wait_recv()
        if c + AHEAD < NC:
            send_forward(c + AHEAD, 0, nb)
        else:
            turn_and_send(c + AHEAD - NC)
        lax.fori_loop(c * jc, (c + 1) * jc, second, 0, unroll=2)
        if c == 1:
            send_l(0)
            turn_own(0)
    for n in range(AHEAD):
        turn_and_send(AHEAD + n)
    send_l(1)
    turn_own(1)

    stores = [pltpu.make_async_copy(out_v, out_hbm, out_sem.at[0])]
    stores[0].start()

    def add_l(jj, carry):
        total = tl_s[dp, jj].astype(F32)
        for s in range(D - 1):
            total = total + tl_r[s, jj].astype(F32)
        gl_v[jj] = total
        return carry

    chip, core = lax.div(dp, 2), lax.rem(dp, 2)
    chips = D // 2

    def last(ii, carry):
        y = gb[ii]
        gi_v[ii] = dot(r_v[ii], y, 1, 0).astype(BF16)
        term = (dot(a_v[ii], y, 1, 1) * scale).astype(BF16)
        for d in range(D):
            tr_s[d % 2, d // 2, ii] = term[d * rows : (d + 1) * rows]
        return carry

    def pair_sum(q, ii):
        return tr_s[core, q, ii].astype(F32) + tr_p[q, ii].astype(F32)

    pairs, sums_r = [], []

    def send_pair(g):
        at = pl.ds(*GROUPS[AHEAD + g][1:])
        copy = remote(
            tr_s.at[1 - core, :, at], tr_p.at[:, at], ps_sem.at[g], pr_sem.at[g],
            "dp", dp + 1 - 2 * core,
        )
        copy.start()
        pairs.append(copy)

    def send_chips(g):
        start, size = GROUPS[AHEAD + g][1:]
        pairs[g].wait_recv()
        step = []
        for s in range(1, chips):
            q = lax.rem(chip + s, chips)

            def add(ii, carry, q=q):
                tr_c[q, ii] = pair_sum(q, ii).astype(BF16)
                return carry

            lax.fori_loop(start, start + size, add, 0, unroll=4)
            copy = remote(
                tr_c.at[q, pl.ds(start, size)],
                tr_r.at[s - 1, pl.ds(start, size)],
                rs_sem.at[g, s - 1],
                rr_sem.at[g, s - 1],
                "dp",
                2 * q + core,
            )
            copy.start()
            step.append(copy)
        sums_r.append(step)

    def add_r(ii, carry):
        total = pair_sum(chip, ii)
        for s in range(chips - 1):
            total = total + tr_r[s, ii].astype(F32)
        gr_v[ii] = total
        return carry

    def finish(g):
        start, size = GROUPS[AHEAD + g][1:]
        for copy in sums_r[g]:
            copy.wait_recv()
        lax.fori_loop(start, start + size, add_r, 0, unroll=4)

    count = len(GROUPS) - AHEAD
    for g in range(count):
        start, size = GROUPS[AHEAD + g][1:]
        for n in range(AHEAD):
            if GROUPS[n][1] == start:
                for copy in back[n]:
                    copy.wait_recv()
        for copy in back[AHEAD + g]:
            copy.wait_recv()
        if g + AHEAD < count:
            turn_and_send(g + 2 * AHEAD)
        lax.fori_loop(start, start + size, last, 0, unroll=2)
        send_pair(g)
        at = pl.ds(start, size)
        stores.append(pltpu.make_async_copy(gi_v.at[at], gi_hbm.at[at], out_sem.at[3 + g]))
        stores[-1].start()
        if g >= 1:
            send_chips(g - 1)
        if g == 1:
            for copy in sums_l:
                copy.wait_recv()
            lax.fori_loop(0, nb, add_l, 0, unroll=2)
            stores.append(pltpu.make_async_copy(gl_v, gl_hbm, out_sem.at[1]))
            stores[-1].start()
    send_chips(count - 1)
    for g in range(count):
        finish(g)
    stores.append(pltpu.make_async_copy(gr_v, gr_hbm, out_sem.at[2]))
    stores[-1].start()

    for step in forward + back + sums_r:
        for copy in step:
            copy.wait_send()
    for copy in sums_l + pairs:
        copy.wait_send()
    for store in stores:
        store.wait()


def write_out(*refs):
    sources, results, held, (in_sem, out_sem) = refs[:4], refs[4:8], refs[8:12], refs[12:]
    pieces = []
    for src, mid, dst, parts in zip(sources, held, results, (2, 2, 1, 1)):
        size = src.shape[0] // parts
        for p in range(parts):
            at = pl.ds(p * size, size)
            n = len(pieces)
            pieces.append((
                pltpu.make_async_copy(src.at[at], mid.at[at], in_sem.at[n]),
                pltpu.make_async_copy(mid.at[at], dst.at[at], out_sem.at[n]),
            ))
    for load, _ in pieces:
        load.start()
    for load, store in pieces:
        load.wait()
        store.start()
    for _, store in pieces:
        store.wait()


def fused(M, D, inputs, cotangent, r_factor, l_factor):
    nb, B = r_factor.shape[1], r_factor.shape[2]
    T = inputs.shape[1]
    rows = B // D
    scale = float(D * T) ** (-0.5)
    NC, H = 4, 2
    half, part, small = nb // 2, nb // 4, nb // 8
    groups = ((0, 0, half), (0, half, half))
    groups += ((1, 0, part), (1, part, part), (1, half, part))
    groups += ((1, half + part, small), (1, half + part + small, small))
    cfg = (M, D, nb, B, T, rows, scale, NC, H, groups)
    count = len(groups) - AHEAD
    sem = pltpu.SemaphoreType.DMA
    flops = 6 * 2 * nb * B * B * T
    results = pl.pallas_call(
        functools.partial(kernel, cfg),
        out_shape=(
            jax.ShapeDtypeStruct((nb, B, T), BF16),
            jax.ShapeDtypeStruct((nb, B, T), BF16),
            jax.ShapeDtypeStruct((nb, rows, B), F32),
            jax.ShapeDtypeStruct((nb, rows, B), F32),
        ),
        in_specs=[pl.BlockSpec(memory_space=pltpu.HBM)] * 4,
        out_specs=[pl.BlockSpec(memory_space=pl.ANY)] * 4,
        scratch_shapes=[
            pltpu.VMEM((nb, B, T), BF16),
            pltpu.VMEM((nb, B, T), BF16),
            pltpu.VMEM((nb, B, B), BF16),
            pltpu.VMEM((nb, B, B), BF16),
            pltpu.VMEM((B * nb, T), F32),
            pltpu.VMEM((B, nb, T), BF16),
            pltpu.VMEM((nb, B, T), BF16),
            pltpu.VMEM((nb * B, T), F32),
            pltpu.VMEM((B, nb, T), BF16),
            pltpu.VMEM((nb, B, T), BF16),
            pltpu.VMEM((nb, B, T), BF16),
            pltpu.VMEM((nb, B, T), BF16),
            pltpu.VMEM((D, nb, rows, B), BF16),
            pltpu.VMEM((D - 1, nb, rows, B), BF16),
            pltpu.VMEM((2, D // 2, nb, rows, B), BF16),
            pltpu.VMEM((D // 2, nb, rows, B), BF16),
            pltpu.VMEM((D // 2, nb, rows, B), BF16),
            pltpu.VMEM((D // 2 - 1, nb, rows, B), BF16),
            pltpu.VMEM((nb, rows, B), F32),
            pltpu.VMEM((nb, rows, B), F32),
            sem((6,)),
            sem((3 + count,)),
            sem((NC * 2, M - 1)),
            sem((NC * 2, M - 1)),
            sem((len(groups), M - 1)),
            sem((len(groups), M - 1)),
            sem((H, D - 1)),
            sem((H, D - 1)),
            sem((count,)),
            sem((count,)),
            sem((count, D // 2 - 1)),
            sem((count, D // 2 - 1)),
        ],
        compiler_params=pltpu.CompilerParams(
            collective_id=0, has_side_effects=True, vmem_limit_bytes=62 * 2**20
        ),
        cost_estimate=pl.CostEstimate(
            flops=flops, bytes_accessed=8 * nb * B * T * 2, transcendentals=nb * B * T
        ),
        name="monarch",
    )(
        inputs.reshape(nb, B, T),
        cotangent.reshape(nb, B, T),
        r_factor[0],
        l_factor[0],
    )
    outputs, grad_inputs, grad_r, grad_l = pl.pallas_call(
        write_out,
        out_shape=[jax.ShapeDtypeStruct(x.shape, x.dtype) for x in results],
        in_specs=[pl.BlockSpec(memory_space=pl.ANY)] * 4,
        out_specs=[pl.BlockSpec(memory_space=pltpu.HBM)] * 4,
        scratch_shapes=[pltpu.VMEM(x.shape, x.dtype) for x in results] + [sem((6,)), sem((6,))],
        compiler_params=pltpu.CompilerParams(vmem_limit_bytes=62 * 2**20),
        name="write_out",
    )(*results)
    return (
        outputs.reshape(nb * B, T),
        grad_inputs.reshape(nb * B, T),
        grad_r[None],
        grad_l[None],
    )


def plain(M, D, inputs, cotangent, r_factor, l_factor):
    nb, B = r_factor.shape[1], r_factor.shape[2]
    T = inputs.shape[1]
    scale = float(D * T) ** (-0.5)
    right, left = r_factor[0], l_factor[0]
    current = inputs.reshape(nb, B, T)
    first_out = jnp.einsum("ikt,ikj->ijt", current, right, preferred_element_type=F32)
    received = lax.all_to_all(
        first_out.astype(BF16), "mp", split_axis=1, concat_axis=0, tiled=True
    )
    pre_act = jnp.einsum("ijt,jim->jmt", received, left, preferred_element_type=F32)
    value, slope = gelu_and_slope(pre_act)
    grad_pre = (cotangent.reshape(nb, B, T).astype(F32) * slope).astype(BF16)
    term_l = jnp.einsum("ijt,jmt->jim", received, grad_pre, preferred_element_type=F32)
    grad_l = lax.psum_scatter(term_l * scale, "dp", scatter_dimension=1, tiled=True)
    grad_first = jnp.einsum("jmt,jim->ijt", grad_pre, left, preferred_element_type=F32)
    returned = lax.all_to_all(
        grad_first.astype(BF16), "mp", split_axis=0, concat_axis=1, tiled=True
    )
    spread = jnp.einsum("ijt,ikj->ikt", returned, right, preferred_element_type=F32)
    term_r = jnp.einsum("ikt,ijt->ikj", current, returned, preferred_element_type=F32)
    grad_r = lax.psum_scatter(term_r * scale, "dp", scatter_dimension=1, tiled=True)
    return (
        value.astype(BF16).reshape(nb * B, T),
        spread.astype(BF16).reshape(nb * B, T),
        grad_r[None],
        grad_l[None],
    )


def solution(mesh):
    M, D = mesh.shape["mp"], mesh.shape["dp"]

    def shards(inputs, cotangent, r_factor, l_factor):
        nb, B = r_factor.shape[1], r_factor.shape[2]
        tiled = nb % 32 == 0 and (B // D) % 16 == 0 and M > 1 and D > 2 and D % 2 == 0
        return (fused if tiled else plain)(M, D, inputs, cotangent, r_factor, l_factor)

    return jax.shard_map(
        shards,
        mesh=mesh,
        in_specs=(P("mp", "dp"), P("mp", "dp"), P(None, "mp"), P(None, "mp")),
        out_specs=(P("mp", "dp"), P("mp", "dp"), P(None, "mp", "dp"), P(None, "mp", "dp")),
        check_vma=False,
    )
```

```python
import functools

import jax
import jax.numpy as jnp
from jax import lax
from jax.experimental import pallas as pl
from jax.experimental.pallas import tpu as pltpu
from jax.sharding import PartitionSpec as P

MESH = pl.DeviceIdType.MESH
F32 = jnp.float32
BF16 = jnp.bfloat16
AHEAD = 2


def dot(left, right, left_dim, right_dim):
    return lax.dot_general(
        left, right, (((left_dim,), (right_dim,)), ((), ())), preferred_element_type=F32
    )


def gelu_and_slope(v):
    c0, c1 = 0.7978845608028654, 0.044715
    square = v * v
    tanh = jnp.tanh(c0 * v * (1.0 + c1 * square))
    half = 0.5 + 0.5 * tanh
    slope = half + 0.5 * v * (1.0 - tanh * tanh) * (c0 + (3.0 * c0 * c1) * square)
    return v * half, slope


def remote(src, dst, send_sem, recv_sem, axis, target):
    return pltpu.make_async_remote_copy(
        src_ref=src,
        dst_ref=dst,
        send_sem=send_sem,
        recv_sem=recv_sem,
        device_id={axis: target},
        device_id_type=MESH,
    )


def kernel(
    cfg,
    a_hbm, g_hbm, r_hbm, l_hbm,
    out_v, gi_v, gr_v, gl_v,
    a_v, g_v, r_v, l_v,
    fo32, fs, fr,
    gf32, gs, gb,
    tl_s, tl_r, tr_s, tr_r,
    in_sem,
    fs_sem, fr_sem, gs_sem, gb_sem,
    ls_sem, lr_sem, rs_sem, rr_sem,
):
    M, D, nb, B, T, rows, scale, NC, H, GROUPS = cfg
    jc, hj = nb // NC, nb // H
    mp, dp = lax.axis_index("mp"), lax.axis_index("dp")

    half = nb // 2
    loads = []
    for src, dst, parts in (
        (a_hbm, a_v, 2), (r_hbm, r_v, 2), (l_hbm, l_v, 1), (g_hbm, g_v, 1)
    ):
        for p in range(parts):
            at = pl.ds(p * (nb // parts), nb // parts)
            loads.append(
                pltpu.make_async_copy(src.at[at], dst.at[at], in_sem.at[len(loads)])
            )
    for n in (0, 2, 1, 3, 4, 5):
        loads[n].start()

    barrier = pltpu.get_barrier_semaphore()
    for s in range(1, M):
        pl.semaphore_signal(
            barrier, inc=1, device_id={"mp": lax.rem(mp + s, M)}, device_id_type=MESH
        )
    for s in range(1, D):
        pl.semaphore_signal(
            barrier, inc=1, device_id={"dp": lax.rem(dp + s, D)}, device_id_type=MESH
        )

    def first(i, carry):
        fo32[pl.ds(i, B, stride=nb), :] = dot(r_v[i], a_v[i], 0, 0)
        return carry

    mine = pl.multiple_of(mp * nb, nb)
    forward = [[] for _ in range(NC)]
    def send_forward(c, start, size):
        for s in range(1, M):
            target = lax.rem(mp + s, M)
            base = target * nb + c * jc

            def pack(j, carry, base=base):
                at = pl.multiple_of((base + j) * nb + start, half)
                fs[base + j, pl.ds(start, size), :] = fo32[pl.ds(at, size), :].astype(BF16)
                return carry

            lax.fori_loop(0, jc, pack, 0, unroll=4)
            slot = c * 2 + start // half
            copy = remote(
                fs.at[pl.ds(base, jc), pl.ds(start, size)],
                fr.at[pl.ds(c * jc, jc), pl.ds(pl.multiple_of(mine + start, half), size)],
                fs_sem.at[slot, s - 1],
                fr_sem.at[slot, s - 1],
                "mp",
                target,
            )
            copy.start()
            forward[c].append(copy)

    for p in range(2):
        loads[p].wait()
        loads[2 + p].wait()
        lax.fori_loop(p * half, (p + 1) * half, first, 0, unroll=4)
        if p == 0:
            pl.semaphore_wait(barrier, (M - 1) + (D - 1))
        for c in range(AHEAD):
            send_forward(c, p * half, half)

    def own(j, carry):
        at = pl.multiple_of((mine + j) * nb, nb)
        fr[j, pl.ds(mine, nb), :] = fo32[pl.ds(at, nb), :].astype(BF16)
        return carry

    lax.fori_loop(0, nb, own, 0, unroll=4)
    loads[4].wait()
    loads[5].wait()

    def second(jj, carry):
        x, left = fr[jj], l_v[jj]
        value, slope = gelu_and_slope(dot(left, x, 0, 0))
        out_v[jj] = value.astype(BF16)
        grad_pre = (g_v[jj].astype(F32) * slope).astype(BF16)
        gf32[pl.ds(pl.multiple_of(jj * B, B), B), :] = dot(left, grad_pre, 1, 0)
        term = (dot(x, grad_pre, 1, 1) * scale).astype(BF16)
        for d in range(D):
            tl_s[d, jj] = term[d * rows : (d + 1) * rows]
        return carry

    back, sums_l = [[] for _ in range(len(GROUPS))], []

    def turn(h, start, size, s):
        base = lax.rem(mp + s, M) * nb + start

        def one(i, carry):
            part = gf32[pl.ds(h * hj * B + base + i, hj, stride=B), :]
            gs[base + i, pl.ds(h * hj, hj), :] = part.astype(BF16)
            return carry

        lax.fori_loop(0, size, one, 0, unroll=4)

    def turn_own(h):
        at_j = pl.multiple_of(mine + h * hj, hj)

        def one(i, carry):
            part = gf32[pl.ds(h * hj * B + mine + i, hj, stride=B), :]
            gb[i, pl.ds(at_j, hj), :] = part.astype(BF16)
            return carry

        lax.fori_loop(0, nb, one, 0, unroll=4)

    def turn_and_send(n):
        h, start, size = GROUPS[n]
        for s in range(1, M):
            turn(h, start, size, s)
            target = lax.rem(mp + s, M)
            at_j = pl.multiple_of(mine + h * hj, hj)
            copy = remote(
                gs.at[pl.ds(target * nb + start, size), pl.ds(h * hj, hj)],
                gb.at[pl.ds(start, size), pl.ds(at_j, hj)],
                gs_sem.at[n, s - 1],
                gb_sem.at[n, s - 1],
                "mp",
                target,
            )
            copy.start()
            back[n].append(copy)

    def send_l(h):
        for s in range(1, D):
            target = lax.rem(dp + s, D)
            copy = remote(
                tl_s.at[target, pl.ds(h * hj, hj)],
                tl_r.at[s - 1, pl.ds(h * hj, hj)],
                ls_sem.at[h, s - 1],
                lr_sem.at[h, s - 1],
                "dp",
                target,
            )
            copy.start()
            sums_l.append(copy)

    for c in range(NC):
        for copy in forward[c]:
            copy.wait_recv()
        if c + AHEAD < NC:
            send_forward(c + AHEAD, 0, nb)
        else:
            turn_and_send(c + AHEAD - NC)
        lax.fori_loop(c * jc, (c + 1) * jc, second, 0, unroll=2)
        if c == 1:
            send_l(0)
            turn_own(0)
    for n in range(AHEAD):
        turn_and_send(AHEAD + n)
    send_l(1)
    turn_own(1)

    def add_l(jj, carry):
        total = tl_s[dp, jj].astype(F32)
        for s in range(D - 1):
            total = total + tl_r[s, jj].astype(F32)
        gl_v[jj] = total
        return carry

    def last(ii, carry):
        y = gb[ii]
        gi_v[ii] = dot(r_v[ii], y, 1, 0).astype(BF16)
        term = (dot(a_v[ii], y, 1, 1) * scale).astype(BF16)
        for d in range(D):
            tr_s[d, ii] = term[d * rows : (d + 1) * rows]
        return carry

    sums_r = []

    def send_r(g):
        at = pl.ds(*GROUPS[AHEAD + g][1:])
        step = []
        for s in range(1, D):
            target = lax.rem(dp + s, D)
            copy = remote(
                tr_s.at[target, at],
                tr_r.at[s - 1, at],
                rs_sem.at[g, s - 1],
                rr_sem.at[g, s - 1],
                "dp",
                target,
            )
            copy.start()
            step.append(copy)
        sums_r.append(step)

    def add_r(ii, carry):
        total = tr_s[dp, ii].astype(F32)
        for s in range(D - 1):
            total = total + tr_r[s, ii].astype(F32)
        gr_v[ii] = total
        return carry

    def finish(g):
        start, size = GROUPS[AHEAD + g][1:]
        for copy in sums_r[g]:
            copy.wait_recv()
        lax.fori_loop(start, start + size, add_r, 0, unroll=4)

    count = len(GROUPS) - AHEAD
    for g in range(count):
        start, size = GROUPS[AHEAD + g][1:]
        for n in range(AHEAD):
            if GROUPS[n][1] == start:
                for copy in back[n]:
                    copy.wait_recv()
        for copy in back[AHEAD + g]:
            copy.wait_recv()
        if g + AHEAD < count:
            turn_and_send(g + 2 * AHEAD)
        lax.fori_loop(start, start + size, last, 0, unroll=2)
        send_r(g)
        if g == 1:
            for copy in sums_l:
                copy.wait_recv()
            lax.fori_loop(0, nb, add_l, 0, unroll=2)
    for g in range(count):
        finish(g)

    for step in forward + back + sums_r:
        for copy in step:
            copy.wait_send()
    for copy in sums_l:
        copy.wait_send()


def write_out(*refs):
    done = refs[8]
    copies = [pltpu.make_async_copy(refs[n], refs[4 + n], done.at[n]) for n in range(4)]
    for copy in copies:
        copy.start()
    for copy in copies:
        copy.wait()


def fused(M, D, inputs, cotangent, r_factor, l_factor):
    nb, B = r_factor.shape[1], r_factor.shape[2]
    T = inputs.shape[1]
    rows = B // D
    scale = float(D * T) ** (-0.5)
    NC, H = 4, 2
    half, part, small = nb // 2, nb // 4, nb // 8
    groups = ((0, 0, half), (0, half, half))
    groups += ((1, 0, part), (1, part, part), (1, half, part))
    groups += ((1, half + part, small), (1, half + part + small, small))
    cfg = (M, D, nb, B, T, rows, scale, NC, H, groups)
    count = len(groups) - AHEAD
    sem = pltpu.SemaphoreType.DMA
    flops = 6 * 2 * nb * B * B * T
    results = pl.pallas_call(
        functools.partial(kernel, cfg),
        out_shape=(
            pltpu.VMEM((nb, B, T), BF16),
            pltpu.VMEM((nb, B, T), BF16),
            pltpu.VMEM((nb, rows, B), F32),
            pltpu.VMEM((nb, rows, B), F32),
        ),
        in_specs=[pl.BlockSpec(memory_space=pltpu.HBM)] * 4,
        out_specs=[pl.BlockSpec(memory_space=pltpu.VMEM)] * 4,
        scratch_shapes=[
            pltpu.VMEM((nb, B, T), BF16),
            pltpu.VMEM((nb, B, T), BF16),
            pltpu.VMEM((nb, B, B), BF16),
            pltpu.VMEM((nb, B, B), BF16),
            pltpu.VMEM((B * nb, T), F32),
            pltpu.VMEM((B, nb, T), BF16),
            pltpu.VMEM((nb, B, T), BF16),
            pltpu.VMEM((nb * B, T), F32),
            pltpu.VMEM((B, nb, T), BF16),
            pltpu.VMEM((nb, B, T), BF16),
            pltpu.VMEM((D, nb, rows, B), BF16),
            pltpu.VMEM((D - 1, nb, rows, B), BF16),
            pltpu.VMEM((D, nb, rows, B), BF16),
            pltpu.VMEM((D - 1, nb, rows, B), BF16),
            sem((6,)),
            sem((NC * 2, M - 1)),
            sem((NC * 2, M - 1)),
            sem((len(groups), M - 1)),
            sem((len(groups), M - 1)),
            sem((H, D - 1)),
            sem((H, D - 1)),
            sem((count, D - 1)),
            sem((count, D - 1)),
        ],
        compiler_params=pltpu.CompilerParams(
            collective_id=0, has_side_effects=True, vmem_limit_bytes=61 * 2**20
        ),
        cost_estimate=pl.CostEstimate(
            flops=flops, bytes_accessed=8 * nb * B * T * 2, transcendentals=nb * B * T
        ),
        name="monarch",
    )(
        inputs.reshape(nb, B, T),
        cotangent.reshape(nb, B, T),
        r_factor[0],
        l_factor[0],
    )
    outputs, grad_inputs, grad_r, grad_l = pl.pallas_call(
        write_out,
        out_shape=[jax.ShapeDtypeStruct(x.shape, x.dtype) for x in results],
        in_specs=[pl.BlockSpec(memory_space=pltpu.VMEM)] * 4,
        out_specs=[pl.BlockSpec(memory_space=pltpu.HBM)] * 4,
        scratch_shapes=[sem((4,))],
        name="write_out",
    )(*results)
    return (
        outputs.reshape(nb * B, T),
        grad_inputs.reshape(nb * B, T),
        grad_r[None],
        grad_l[None],
    )


def plain(M, D, inputs, cotangent, r_factor, l_factor):
    nb, B = r_factor.shape[1], r_factor.shape[2]
    T = inputs.shape[1]
    scale = float(D * T) ** (-0.5)
    right, left = r_factor[0], l_factor[0]
    current = inputs.reshape(nb, B, T)
    first_out = jnp.einsum("ikt,ikj->ijt", current, right, preferred_element_type=F32)
    received = lax.all_to_all(
        first_out.astype(BF16), "mp", split_axis=1, concat_axis=0, tiled=True
    )
    pre_act = jnp.einsum("ijt,jim->jmt", received, left, preferred_element_type=F32)
    value, slope = gelu_and_slope(pre_act)
    grad_pre = (cotangent.reshape(nb, B, T).astype(F32) * slope).astype(BF16)
    term_l = jnp.einsum("ijt,jmt->jim", received, grad_pre, preferred_element_type=F32)
    grad_l = lax.psum_scatter(term_l * scale, "dp", scatter_dimension=1, tiled=True)
    grad_first = jnp.einsum("jmt,jim->ijt", grad_pre, left, preferred_element_type=F32)
    returned = lax.all_to_all(
        grad_first.astype(BF16), "mp", split_axis=0, concat_axis=1, tiled=True
    )
    spread = jnp.einsum("ijt,ikj->ikt", returned, right, preferred_element_type=F32)
    term_r = jnp.einsum("ikt,ijt->ikj", current, returned, preferred_element_type=F32)
    grad_r = lax.psum_scatter(term_r * scale, "dp", scatter_dimension=1, tiled=True)
    return (
        value.astype(BF16).reshape(nb * B, T),
        spread.astype(BF16).reshape(nb * B, T),
        grad_r[None],
        grad_l[None],
    )


def solution(mesh):
    M, D = mesh.shape["mp"], mesh.shape["dp"]

    def shards(inputs, cotangent, r_factor, l_factor):
        nb, B = r_factor.shape[1], r_factor.shape[2]
        tiled = nb % 32 == 0 and (B // D) % 16 == 0 and M > 1 and D > 1
        return (fused if tiled else plain)(M, D, inputs, cotangent, r_factor, l_factor)

    return jax.shard_map(
        shards,
        mesh=mesh,
        in_specs=(P("mp", "dp"), P("mp", "dp"), P(None, "mp"), P(None, "mp")),
        out_specs=(P("mp", "dp"), P("mp", "dp"), P(None, "mp", "dp"), P(None, "mp", "dp")),
        check_vma=False,
    )
```

```python
import functools

import jax
import jax.numpy as jnp
from jax import lax
from jax.experimental import pallas as pl
from jax.experimental.pallas import tpu as pltpu
from jax.sharding import PartitionSpec as P

MESH = pl.DeviceIdType.MESH
F32 = jnp.float32
BF16 = jnp.bfloat16
AHEAD = 3
BACK = 2


def dot(left, right, left_dim, right_dim):
    return lax.dot_general(
        left, right, (((left_dim,), (right_dim,)), ((), ())), preferred_element_type=F32
    )


def gelu_and_slope(v):
    c0, c1 = 0.7978845608028654, 0.044715
    square = v * v
    tanh = jnp.tanh(c0 * v * (1.0 + c1 * square))
    half = 0.5 + 0.5 * tanh
    slope = half + 0.5 * v * (1.0 - tanh * tanh) * (c0 + (3.0 * c0 * c1) * square)
    return v * half, slope


def partners(me, size):
    if size == 4:
        return [lax.rem(me + 2, 4), 3 - me, me + 1 - 2 * lax.rem(me, 2)]
    return [lax.rem(me + s, size) for s in range(1, size)]


def remote(src, dst, send_sem, recv_sem, axis, target):
    return pltpu.make_async_remote_copy(
        src_ref=src,
        dst_ref=dst,
        send_sem=send_sem,
        recv_sem=recv_sem,
        device_id={axis: target},
        device_id_type=MESH,
    )


def kernel(
    cfg,
    a_hbm, g_hbm, r_hbm, l_hbm,
    out_v, gi_v, gr_v, gl_v,
    a_v, g_v, r_v, l_v,
    fo32, fs, fr,
    gf32, gs, gb,
    tl_s, tl_r, tr_s, tr_r,
    in_sem,
    fs_sem, fr_sem, gs_sem, gb_sem,
    ls_sem, lr_sem, rs_sem, rr_sem,
):
    M, D, nb, B, T, rows, scale, NC, H, GROUPS = cfg
    jc, hj = nb // NC, nb // H
    mp, dp = lax.axis_index("mp"), lax.axis_index("dp")

    half = nb // 2
    others = partners(mp, M)
    early = sum(1 for group in GROUPS if group[0] == 0)
    loads = []
    for src, dst, parts in (
        (a_hbm, a_v, 2), (r_hbm, r_v, 2), (l_hbm, l_v, 1), (g_hbm, g_v, 1)
    ):
        for p in range(parts):
            at = pl.ds(p * (nb // parts), nb // parts)
            loads.append(
                pltpu.make_async_copy(src.at[at], dst.at[at], in_sem.at[len(loads)])
            )
    for n in (0, 2, 1, 3, 4, 5):
        loads[n].start()

    barrier = pltpu.get_barrier_semaphore()
    for s in range(1, M):
        pl.semaphore_signal(
            barrier, inc=1, device_id={"mp": lax.rem(mp + s, M)}, device_id_type=MESH
        )
    for s in range(1, D):
        pl.semaphore_signal(
            barrier, inc=1, device_id={"dp": lax.rem(dp + s, D)}, device_id_type=MESH
        )

    def first(i, carry):
        fo32[pl.ds(i, B, stride=nb), :] = dot(r_v[i], a_v[i], 0, 0)
        return carry

    mine = pl.multiple_of(mp * nb, nb)
    forward = [[] for _ in range(NC)]
    def send_forward(c, start, size):
        for s, target in enumerate(others, 1):
            base = target * nb + c * jc

            def pack(j, carry, base=base):
                at = pl.multiple_of((base + j) * nb + start, half)
                fs[base + j, pl.ds(start, size), :] = fo32[pl.ds(at, size), :].astype(BF16)
                return carry

            lax.fori_loop(0, jc, pack, 0, unroll=4)
            slot = c * 2 + start // half
            copy = remote(
                fs.at[pl.ds(base, jc), pl.ds(start, size)],
                fr.at[pl.ds(c * jc, jc), pl.ds(pl.multiple_of(mine + start, half), size)],
                fs_sem.at[slot, s - 1],
                fr_sem.at[slot, s - 1],
                "mp",
                target,
            )
            copy.start()
            forward[c].append(copy)

    for p in range(2):
        loads[p].wait()
        loads[2 + p].wait()
        lax.fori_loop(p * half, (p + 1) * half, first, 0, unroll=4)
        if p == 0:
            pl.semaphore_wait(barrier, (M - 1) + (D - 1))
        for c in range(AHEAD):
            send_forward(c, p * half, half)

    def own(j, carry):
        at = pl.multiple_of((mine + j) * nb, nb)
        fr[j, pl.ds(mine, nb), :] = fo32[pl.ds(at, nb), :].astype(BF16)
        return carry

    lax.fori_loop(0, nb, own, 0, unroll=4)
    loads[4].wait()
    loads[5].wait()

    def second(jj, carry):
        x, left = fr[jj], l_v[jj]
        value, slope = gelu_and_slope(dot(left, x, 0, 0))
        out_v[jj] = value.astype(BF16)
        grad_pre = (g_v[jj].astype(F32) * slope).astype(BF16)
        gf32[pl.ds(pl.multiple_of(jj * B, B), B), :] = dot(left, grad_pre, 1, 0)
        term = (dot(x, grad_pre, 1, 1) * scale).astype(BF16)
        for d in range(D):
            tl_s[d, jj] = term[d * rows : (d + 1) * rows]
        return carry

    back, sums_l = [[] for _ in range(len(GROUPS))], []

    def turn(h, start, size, target):
        base = target * nb + start

        def one(i, carry):
            part = gf32[pl.ds(h * hj * B + base + i, hj, stride=B), :]
            gs[base + i, pl.ds(h * hj, hj), :] = part.astype(BF16)
            return carry

        lax.fori_loop(0, size, one, 0, unroll=4)

    def turn_own(h):
        at_j = pl.multiple_of(mine + h * hj, hj)

        def one(i, carry):
            part = gf32[pl.ds(h * hj * B + mine + i, hj, stride=B), :]
            gb[i, pl.ds(at_j, hj), :] = part.astype(BF16)
            return carry

        lax.fori_loop(0, nb, one, 0, unroll=4)

    def turn_and_send(n):
        h, start, size = GROUPS[n]
        for s, target in enumerate(others, 1):
            turn(h, start, size, target)
            at_j = pl.multiple_of(mine + h * hj, hj)
            copy = remote(
                gs.at[pl.ds(target * nb + start, size), pl.ds(h * hj, hj)],
                gb.at[pl.ds(start, size), pl.ds(at_j, hj)],
                gs_sem.at[n, s - 1],
                gb_sem.at[n, s - 1],
                "mp",
                target,
            )
            copy.start()
            back[n].append(copy)

    def send_l(h):
        for s in range(1, D):
            target = lax.rem(dp + s, D)
            copy = remote(
                tl_s.at[target, pl.ds(h * hj, hj)],
                tl_r.at[s - 1, pl.ds(h * hj, hj)],
                ls_sem.at[h, s - 1],
                lr_sem.at[h, s - 1],
                "dp",
                target,
            )
            copy.start()
            sums_l.append(copy)

    for c in range(NC):
        for copy in forward[c]:
            copy.wait_recv()
        if c + AHEAD < NC:
            send_forward(c + AHEAD, 0, nb)
        else:
            turn_and_send(c + AHEAD - NC)
            if c == NC - 1:
                for n in range(AHEAD, early):
                    turn_and_send(n)
        lax.fori_loop(c * jc, (c + 1) * jc, second, 0, unroll=2)
        if c == NC // H - 1:
            send_l(0)
            turn_own(0)
    for n in range(BACK):
        turn_and_send(early + n)
    send_l(1)
    turn_own(1)

    def add_l(jj, carry):
        total = tl_s[dp, jj].astype(F32)
        for s in range(D - 1):
            total = total + tl_r[s, jj].astype(F32)
        gl_v[jj] = total
        return carry

    def last(ii, carry):
        y = gb[ii]
        gi_v[ii] = dot(r_v[ii], y, 1, 0).astype(BF16)
        term = (dot(a_v[ii], y, 1, 1) * scale).astype(BF16)
        for d in range(D):
            tr_s[d, ii] = term[d * rows : (d + 1) * rows]
        return carry

    sums_r = []

    def send_r(g):
        at = pl.ds(*GROUPS[early + g][1:])
        step = []
        for s in range(1, D):
            target = lax.rem(dp + s, D)
            copy = remote(
                tr_s.at[target, at],
                tr_r.at[s - 1, at],
                rs_sem.at[g, s - 1],
                rr_sem.at[g, s - 1],
                "dp",
                target,
            )
            copy.start()
            step.append(copy)
        sums_r.append(step)

    def add_r(ii, carry):
        total = tr_s[dp, ii].astype(F32)
        for s in range(D - 1):
            total = total + tr_r[s, ii].astype(F32)
        gr_v[ii] = total
        return carry

    def finish(g):
        start, size = GROUPS[early + g][1:]
        for copy in sums_r[g]:
            copy.wait_recv()
        lax.fori_loop(start, start + size, add_r, 0, unroll=4)

    count = len(GROUPS) - early
    for g in range(count):
        start, size = GROUPS[early + g][1:]
        for n in range(early):
            if GROUPS[n][1] == start:
                for copy in back[n]:
                    copy.wait_recv()
        for copy in back[early + g]:
            copy.wait_recv()
        if g + BACK < count:
            turn_and_send(early + g + BACK)
        lax.fori_loop(start, start + size, last, 0, unroll=2)
        send_r(g)
        if g == 1:
            for copy in sums_l:
                copy.wait_recv()
            lax.fori_loop(0, nb, add_l, 0, unroll=2)
    for g in range(count):
        finish(g)

    for step in forward + back + sums_r:
        for copy in step:
            copy.wait_send()
    for copy in sums_l:
        copy.wait_send()


def write_out(*refs):
    done = refs[8]
    copies = [pltpu.make_async_copy(refs[n], refs[4 + n], done.at[n]) for n in range(4)]
    for copy in copies:
        copy.start()
    for copy in copies:
        copy.wait()


def fused(M, D, inputs, cotangent, r_factor, l_factor):
    nb, B = r_factor.shape[1], r_factor.shape[2]
    T = inputs.shape[1]
    rows = B // D
    scale = float(D * T) ** (-0.5)
    NC, H = 8, 2
    half, part, small = nb // 2, nb // 4, nb // 8
    groups = tuple((0, n * part, part) for n in range(4))
    groups += ((1, 0, part), (1, part, part), (1, half, part))
    groups += ((1, half + part, small), (1, half + part + small, small))
    cfg = (M, D, nb, B, T, rows, scale, NC, H, groups)
    count = sum(1 for group in groups if group[0] == 1)
    sem = pltpu.SemaphoreType.DMA
    flops = 6 * 2 * nb * B * B * T
    results = pl.pallas_call(
        functools.partial(kernel, cfg),
        out_shape=(
            pltpu.VMEM((nb, B, T), BF16),
            pltpu.VMEM((nb, B, T), BF16),
            pltpu.VMEM((nb, rows, B), F32),
            pltpu.VMEM((nb, rows, B), F32),
        ),
        in_specs=[pl.BlockSpec(memory_space=pltpu.HBM)] * 4,
        out_specs=[pl.BlockSpec(memory_space=pltpu.VMEM)] * 4,
        scratch_shapes=[
            pltpu.VMEM((nb, B, T), BF16),
            pltpu.VMEM((nb, B, T), BF16),
            pltpu.VMEM((nb, B, B), BF16),
            pltpu.VMEM((nb, B, B), BF16),
            pltpu.VMEM((B * nb, T), F32),
            pltpu.VMEM((B, nb, T), BF16),
            pltpu.VMEM((nb, B, T), BF16),
            pltpu.VMEM((nb * B, T), F32),
            pltpu.VMEM((B, nb, T), BF16),
            pltpu.VMEM((nb, B, T), BF16),
            pltpu.VMEM((D, nb, rows, B), BF16),
            pltpu.VMEM((D - 1, nb, rows, B), BF16),
            pltpu.VMEM((D, nb, rows, B), BF16),
            pltpu.VMEM((D - 1, nb, rows, B), BF16),
            sem((6,)),
            sem((NC * 2, M - 1)),
            sem((NC * 2, M - 1)),
            sem((len(groups), M - 1)),
            sem((len(groups), M - 1)),
            sem((H, D - 1)),
            sem((H, D - 1)),
            sem((count, D - 1)),
            sem((count, D - 1)),
        ],
        compiler_params=pltpu.CompilerParams(
            collective_id=0, has_side_effects=True, vmem_limit_bytes=61 * 2**20
        ),
        cost_estimate=pl.CostEstimate(
            flops=flops, bytes_accessed=8 * nb * B * T * 2, transcendentals=nb * B * T
        ),
        name="monarch",
    )(
        inputs.reshape(nb, B, T),
        cotangent.reshape(nb, B, T),
        r_factor[0],
        l_factor[0],
    )
    outputs, grad_inputs, grad_r, grad_l = pl.pallas_call(
        write_out,
        out_shape=[jax.ShapeDtypeStruct(x.shape, x.dtype) for x in results],
        in_specs=[pl.BlockSpec(memory_space=pl.ANY)] * 4,
        out_specs=[pl.BlockSpec(memory_space=pltpu.HBM)] * 4,
        scratch_shapes=[sem((4,))],
        compiler_params=pltpu.CompilerParams(vmem_limit_bytes=4 * 2**20),
        name="write_out",
    )(*results)
    return (
        outputs.reshape(nb * B, T),
        grad_inputs.reshape(nb * B, T),
        grad_r[None],
        grad_l[None],
    )


def plain(M, D, inputs, cotangent, r_factor, l_factor):
    nb, B = r_factor.shape[1], r_factor.shape[2]
    T = inputs.shape[1]
    scale = float(D * T) ** (-0.5)
    right, left = r_factor[0], l_factor[0]
    current = inputs.reshape(nb, B, T)
    first_out = jnp.einsum("ikt,ikj->ijt", current, right, preferred_element_type=F32)
    received = lax.all_to_all(
        first_out.astype(BF16), "mp", split_axis=1, concat_axis=0, tiled=True
    )
    pre_act = jnp.einsum("ijt,jim->jmt", received, left, preferred_element_type=F32)
    value, slope = gelu_and_slope(pre_act)
    grad_pre = (cotangent.reshape(nb, B, T).astype(F32) * slope).astype(BF16)
    term_l = jnp.einsum("ijt,jmt->jim", received, grad_pre, preferred_element_type=F32)
    grad_l = lax.psum_scatter(term_l * scale, "dp", scatter_dimension=1, tiled=True)
    grad_first = jnp.einsum("jmt,jim->ijt", grad_pre, left, preferred_element_type=F32)
    returned = lax.all_to_all(
        grad_first.astype(BF16), "mp", split_axis=0, concat_axis=1, tiled=True
    )
    spread = jnp.einsum("ijt,ikj->ikt", returned, right, preferred_element_type=F32)
    term_r = jnp.einsum("ikt,ijt->ikj", current, returned, preferred_element_type=F32)
    grad_r = lax.psum_scatter(term_r * scale, "dp", scatter_dimension=1, tiled=True)
    return (
        value.astype(BF16).reshape(nb * B, T),
        spread.astype(BF16).reshape(nb * B, T),
        grad_r[None],
        grad_l[None],
    )


def solution(mesh):
    M, D = mesh.shape["mp"], mesh.shape["dp"]

    def shards(inputs, cotangent, r_factor, l_factor):
        nb, B = r_factor.shape[1], r_factor.shape[2]
        tiled = nb % 32 == 0 and (B // D) % 16 == 0 and M > 1 and D > 1
        return (fused if tiled else plain)(M, D, inputs, cotangent, r_factor, l_factor)

    return jax.shard_map(
        shards,
        mesh=mesh,
        in_specs=(P("mp", "dp"), P("mp", "dp"), P(None, "mp"), P(None, "mp")),
        out_specs=(P("mp", "dp"), P("mp", "dp"), P(None, "mp", "dp"), P(None, "mp", "dp")),
        check_vma=False,
    )
```

```python
import functools

import jax
import jax.numpy as jnp
from jax import lax
from jax.experimental import pallas as pl
from jax.experimental.pallas import tpu as pltpu
from jax.sharding import PartitionSpec as P

MESH = pl.DeviceIdType.MESH
F32 = jnp.float32
BF16 = jnp.bfloat16
AHEAD = 2
BACK = 2


def dot(left, right, left_dim, right_dim):
    return lax.dot_general(
        left, right, (((left_dim,), (right_dim,)), ((), ())), preferred_element_type=F32
    )


def gelu_and_slope(v):
    c0, c1 = 0.7978845608028654, 0.044715
    square = v * v
    tanh = jnp.tanh(c0 * v * (1.0 + c1 * square))
    half = 0.5 + 0.5 * tanh
    slope = half + 0.5 * v * (1.0 - tanh * tanh) * (c0 + (3.0 * c0 * c1) * square)
    return v * half, slope


def partners(me, size):
    if size == 4:
        return [lax.rem(me + 2, 4), 3 - me, me + 1 - 2 * lax.rem(me, 2)]
    return [lax.rem(me + s, size) for s in range(1, size)]


def remote(src, dst, send_sem, recv_sem, axis, target):
    return pltpu.make_async_remote_copy(
        src_ref=src,
        dst_ref=dst,
        send_sem=send_sem,
        recv_sem=recv_sem,
        device_id={axis: target},
        device_id_type=MESH,
    )


def kernel(
    cfg,
    a_hbm, g_hbm, r_hbm, l_hbm,
    out_v, gi_v, gr_v, gl_v,
    a_v, g_v, r_v, l_v,
    fo32, fs, fr,
    gf32, gs, gb,
    tl_s, tl_r, tr_s, tr_r,
    in_sem,
    fs_sem, fr_sem, gs_sem, gb_sem,
    ls_sem, lr_sem, rs_sem, rr_sem,
):
    M, D, nb, B, T, rows, scale, NC, H, GROUPS = cfg
    jc, hj = nb // NC, nb // H
    mp, dp = lax.axis_index("mp"), lax.axis_index("dp")

    half = nb // 2
    others = partners(mp, M)
    early = sum(1 for group in GROUPS if group[0] == 0)
    loads = []
    for src, dst, parts in (
        (a_hbm, a_v, 2), (r_hbm, r_v, 2), (l_hbm, l_v, 1), (g_hbm, g_v, 1)
    ):
        for p in range(parts):
            at = pl.ds(p * (nb // parts), nb // parts)
            loads.append(
                pltpu.make_async_copy(src.at[at], dst.at[at], in_sem.at[len(loads)])
            )
    for n in (0, 2, 1, 3, 4, 5):
        loads[n].start()

    barrier = pltpu.get_barrier_semaphore()
    for s in range(1, M):
        pl.semaphore_signal(
            barrier, inc=1, device_id={"mp": lax.rem(mp + s, M)}, device_id_type=MESH
        )
    for s in range(1, D):
        pl.semaphore_signal(
            barrier, inc=1, device_id={"dp": lax.rem(dp + s, D)}, device_id_type=MESH
        )

    def first(i, carry):
        fo32[pl.ds(i, B, stride=nb), :] = dot(r_v[i], a_v[i], 0, 0)
        return carry

    mine = pl.multiple_of(mp * nb, nb)
    forward = [[] for _ in range(NC)]
    def send_forward(c, start, size):
        for s, target in enumerate(others, 1):
            base = target * nb + c * jc

            def pack(j, carry, base=base):
                at = pl.multiple_of((base + j) * nb + start, half)
                fs[base + j, pl.ds(start, size), :] = fo32[pl.ds(at, size), :].astype(BF16)
                return carry

            lax.fori_loop(0, jc, pack, 0, unroll=8)
            slot = c * 2 + start // half
            copy = remote(
                fs.at[pl.ds(base, jc), pl.ds(start, size)],
                fr.at[pl.ds(c * jc, jc), pl.ds(pl.multiple_of(mine + start, half), size)],
                fs_sem.at[slot, s - 1],
                fr_sem.at[slot, s - 1],
                "mp",
                target,
            )
            copy.start()
            forward[c].append(copy)

    for p in range(2):
        loads[p].wait()
        loads[2 + p].wait()
        lax.fori_loop(p * half, (p + 1) * half, first, 0, unroll=8)
        if p == 0:
            pl.semaphore_wait(barrier, (M - 1) + (D - 1))
        for c in range(AHEAD):
            send_forward(c, p * half, half)

    def own(j, carry):
        at = pl.multiple_of((mine + j) * nb, nb)
        fr[j, pl.ds(mine, nb), :] = fo32[pl.ds(at, nb), :].astype(BF16)
        return carry

    lax.fori_loop(0, nb, own, 0, unroll=4)
    loads[4].wait()
    loads[5].wait()

    def second(jj, carry):
        x, left = fr[jj], l_v[jj]
        value, slope = gelu_and_slope(dot(left, x, 0, 0))
        out_v[jj] = value.astype(BF16)
        grad_pre = (g_v[jj].astype(F32) * slope).astype(BF16)
        gf32[pl.ds(pl.multiple_of(jj * B, B), B), :] = dot(left, grad_pre, 1, 0)
        term = (dot(x, grad_pre, 1, 1) * scale).astype(BF16)
        for d in range(D):
            tl_s[d, jj] = term[d * rows : (d + 1) * rows]
        return carry

    back, sums_l = [[] for _ in range(len(GROUPS))], []

    def turn(h, start, size, target):
        base = target * nb + start

        def one(i, carry):
            part = gf32[pl.ds(h * hj * B + base + i, hj, stride=B), :]
            gs[base + i, pl.ds(h * hj, hj), :] = part.astype(BF16)
            return carry

        lax.fori_loop(0, size, one, 0, unroll=8)

    def turn_own(h):
        at_j = pl.multiple_of(mine + h * hj, hj)

        def one(i, carry):
            part = gf32[pl.ds(h * hj * B + mine + i, hj, stride=B), :]
            gb[i, pl.ds(at_j, hj), :] = part.astype(BF16)
            return carry

        lax.fori_loop(0, nb, one, 0, unroll=8)

    def turn_and_send(n):
        h, start, size = GROUPS[n]
        for s, target in enumerate(others, 1):
            turn(h, start, size, target)
            at_j = pl.multiple_of(mine + h * hj, hj)
            copy = remote(
                gs.at[pl.ds(target * nb + start, size), pl.ds(h * hj, hj)],
                gb.at[pl.ds(start, size), pl.ds(at_j, hj)],
                gs_sem.at[n, s - 1],
                gb_sem.at[n, s - 1],
                "mp",
                target,
            )
            copy.start()
            back[n].append(copy)

    def send_l(h):
        for s in range(1, D):
            target = lax.rem(dp + s, D)
            copy = remote(
                tl_s.at[target, pl.ds(h * hj, hj)],
                tl_r.at[s - 1, pl.ds(h * hj, hj)],
                ls_sem.at[h, s - 1],
                lr_sem.at[h, s - 1],
                "dp",
                target,
            )
            copy.start()
            sums_l.append(copy)

    for c in range(NC):
        for copy in forward[c]:
            copy.wait_recv()
        if c + AHEAD < NC:
            send_forward(c + AHEAD, 0, nb)
        else:
            turn_and_send(c + AHEAD - NC)
            if c == NC - 1:
                for n in range(AHEAD, early):
                    turn_and_send(n)
        lax.fori_loop(c * jc, (c + 1) * jc, second, 0, unroll=4)
        if c == NC // H - 1:
            send_l(0)
            turn_own(0)
    for n in range(BACK):
        turn_and_send(early + n)
    send_l(1)
    turn_own(1)

    def add_l(jj, carry):
        total = tl_s[dp, jj].astype(F32)
        for s in range(D - 1):
            total = total + tl_r[s, jj].astype(F32)
        gl_v[jj] = total
        return carry

    def last(ii, carry):
        y = gb[ii]
        gi_v[ii] = dot(r_v[ii], y, 1, 0).astype(BF16)
        term = (dot(a_v[ii], y, 1, 1) * scale).astype(BF16)
        for d in range(D):
            tr_s[d, ii] = term[d * rows : (d + 1) * rows]
        return carry

    sums_r = []

    def send_r(g):
        at = pl.ds(*GROUPS[early + g][1:])
        step = []
        for s in range(1, D):
            target = lax.rem(dp + s, D)
            copy = remote(
                tr_s.at[target, at],
                tr_r.at[s - 1, at],
                rs_sem.at[g, s - 1],
                rr_sem.at[g, s - 1],
                "dp",
                target,
            )
            copy.start()
            step.append(copy)
        sums_r.append(step)

    def add_r(ii, carry):
        total = tr_s[dp, ii].astype(F32)
        for s in range(D - 1):
            total = total + tr_r[s, ii].astype(F32)
        gr_v[ii] = total
        return carry

    def finish(g):
        start, size = GROUPS[early + g][1:]
        for copy in sums_r[g]:
            copy.wait_recv()
        lax.fori_loop(start, start + size, add_r, 0, unroll=4)

    count = len(GROUPS) - early
    for g in range(count):
        start, size = GROUPS[early + g][1:]
        for n in range(early):
            if GROUPS[n][1] == start:
                for copy in back[n]:
                    copy.wait_recv()
        for copy in back[early + g]:
            copy.wait_recv()
        if g + BACK < count:
            turn_and_send(early + g + BACK)
        lax.fori_loop(start, start + size, last, 0, unroll=4)
        send_r(g)
        if g == 1:
            for copy in sums_l:
                copy.wait_recv()
            lax.fori_loop(0, nb, add_l, 0, unroll=2)
    for g in range(count):
        finish(g)

    for step in forward + back + sums_r:
        for copy in step:
            copy.wait_send()
    for copy in sums_l:
        copy.wait_send()


def write_out(*refs):
    done = refs[8]
    copies = [pltpu.make_async_copy(refs[n], refs[4 + n], done.at[n]) for n in range(4)]
    for copy in copies:
        copy.start()
    for copy in copies:
        copy.wait()


def fused(M, D, inputs, cotangent, r_factor, l_factor):
    nb, B = r_factor.shape[1], r_factor.shape[2]
    T = inputs.shape[1]
    rows = B // D
    scale = float(D * T) ** (-0.5)
    NC, H = 4, 2
    half, part, small = nb // 2, nb // 4, nb // 8
    groups = ((0, 0, half), (0, half, half))
    groups += ((1, 0, part), (1, part, part), (1, half, part))
    groups += ((1, half + part, small), (1, half + part + small, small))
    cfg = (M, D, nb, B, T, rows, scale, NC, H, groups)
    count = sum(1 for group in groups if group[0] == 1)
    sem = pltpu.SemaphoreType.DMA
    flops = 6 * 2 * nb * B * B * T
    results = pl.pallas_call(
        functools.partial(kernel, cfg),
        out_shape=(
            pltpu.VMEM((nb, B, T), BF16),
            pltpu.VMEM((nb, B, T), BF16),
            pltpu.VMEM((nb, rows, B), F32),
            pltpu.VMEM((nb, rows, B), F32),
        ),
        in_specs=[pl.BlockSpec(memory_space=pltpu.HBM)] * 4,
        out_specs=[pl.BlockSpec(memory_space=pltpu.VMEM)] * 4,
        scratch_shapes=[
            pltpu.VMEM((nb, B, T), BF16),
            pltpu.VMEM((nb, B, T), BF16),
            pltpu.VMEM((nb, B, B), BF16),
            pltpu.VMEM((nb, B, B), BF16),
            pltpu.VMEM((B * nb, T), F32),
            pltpu.VMEM((B, nb, T), BF16),
            pltpu.VMEM((nb, B, T), BF16),
            pltpu.VMEM((nb * B, T), F32),
            pltpu.VMEM((B, nb, T), BF16),
            pltpu.VMEM((nb, B, T), BF16),
            pltpu.VMEM((D, nb, rows, B), BF16),
            pltpu.VMEM((D - 1, nb, rows, B), BF16),
            pltpu.VMEM((D, nb, rows, B), BF16),
            pltpu.VMEM((D - 1, nb, rows, B), BF16),
            sem((6,)),
            sem((NC * 2, M - 1)),
            sem((NC * 2, M - 1)),
            sem((len(groups), M - 1)),
            sem((len(groups), M - 1)),
            sem((H, D - 1)),
            sem((H, D - 1)),
            sem((count, D - 1)),
            sem((count, D - 1)),
        ],
        compiler_params=pltpu.CompilerParams(
            collective_id=0, has_side_effects=True, vmem_limit_bytes=61 * 2**20
        ),
        cost_estimate=pl.CostEstimate(
            flops=flops, bytes_accessed=8 * nb * B * T * 2, transcendentals=nb * B * T
        ),
        name="monarch",
    )(
        inputs.reshape(nb, B, T),
        cotangent.reshape(nb, B, T),
        r_factor[0],
        l_factor[0],
    )
    outputs, grad_inputs, grad_r, grad_l = pl.pallas_call(
        write_out,
        out_shape=[jax.ShapeDtypeStruct(x.shape, x.dtype) for x in results],
        in_specs=[pl.BlockSpec(memory_space=pl.ANY)] * 4,
        out_specs=[pl.BlockSpec(memory_space=pltpu.HBM)] * 4,
        scratch_shapes=[sem((4,))],
        compiler_params=pltpu.CompilerParams(vmem_limit_bytes=4 * 2**20),
        name="write_out",
    )(*results)
    return (
        outputs.reshape(nb * B, T),
        grad_inputs.reshape(nb * B, T),
        grad_r[None],
        grad_l[None],
    )


def plain(M, D, inputs, cotangent, r_factor, l_factor):
    nb, B = r_factor.shape[1], r_factor.shape[2]
    T = inputs.shape[1]
    scale = float(D * T) ** (-0.5)
    right, left = r_factor[0], l_factor[0]
    current = inputs.reshape(nb, B, T)
    first_out = jnp.einsum("ikt,ikj->ijt", current, right, preferred_element_type=F32)
    received = lax.all_to_all(
        first_out.astype(BF16), "mp", split_axis=1, concat_axis=0, tiled=True
    )
    pre_act = jnp.einsum("ijt,jim->jmt", received, left, preferred_element_type=F32)
    value, slope = gelu_and_slope(pre_act)
    grad_pre = (cotangent.reshape(nb, B, T).astype(F32) * slope).astype(BF16)
    term_l = jnp.einsum("ijt,jmt->jim", received, grad_pre, preferred_element_type=F32)
    grad_l = lax.psum_scatter(term_l * scale, "dp", scatter_dimension=1, tiled=True)
    grad_first = jnp.einsum("jmt,jim->ijt", grad_pre, left, preferred_element_type=F32)
    returned = lax.all_to_all(
        grad_first.astype(BF16), "mp", split_axis=0, concat_axis=1, tiled=True
    )
    spread = jnp.einsum("ijt,ikj->ikt", returned, right, preferred_element_type=F32)
    term_r = jnp.einsum("ikt,ijt->ikj", current, returned, preferred_element_type=F32)
    grad_r = lax.psum_scatter(term_r * scale, "dp", scatter_dimension=1, tiled=True)
    return (
        value.astype(BF16).reshape(nb * B, T),
        spread.astype(BF16).reshape(nb * B, T),
        grad_r[None],
        grad_l[None],
    )


def solution(mesh):
    M, D = mesh.shape["mp"], mesh.shape["dp"]

    def shards(inputs, cotangent, r_factor, l_factor):
        nb, B = r_factor.shape[1], r_factor.shape[2]
        tiled = nb % 32 == 0 and (B // D) % 16 == 0 and M > 1 and D > 1
        return (fused if tiled else plain)(M, D, inputs, cotangent, r_factor, l_factor)

    return jax.shard_map(
        shards,
        mesh=mesh,
        in_specs=(P("mp", "dp"), P("mp", "dp"), P(None, "mp"), P(None, "mp")),
        out_specs=(P("mp", "dp"), P("mp", "dp"), P(None, "mp", "dp"), P(None, "mp", "dp")),
        check_vma=False,
    )
```

```python
import functools

import jax
import jax.numpy as jnp
from jax import lax
from jax.experimental import pallas as pl
from jax.experimental.pallas import tpu as pltpu
from jax.sharding import PartitionSpec as P

MESH = pl.DeviceIdType.MESH
F32 = jnp.float32
BF16 = jnp.bfloat16
AHEAD = 2
BACK = 2


def dot(left, right, left_dim, right_dim):
    return lax.dot_general(
        left, right, (((left_dim,), (right_dim,)), ((), ())), preferred_element_type=F32
    )


def gelu_and_slope(v):
    c0, c1 = 0.7978845608028654, 0.044715
    square = v * v
    tanh = jnp.tanh(c0 * v * (1.0 + c1 * square))
    half = 0.5 + 0.5 * tanh
    slope = half + 0.5 * v * (1.0 - tanh * tanh) * (c0 + (3.0 * c0 * c1) * square)
    return v * half, slope


def remote(src, dst, send_sem, recv_sem, axis, target):
    return pltpu.make_async_remote_copy(
        src_ref=src,
        dst_ref=dst,
        send_sem=send_sem,
        recv_sem=recv_sem,
        device_id={axis: target},
        device_id_type=MESH,
    )


def kernel(
    cfg,
    a_hbm, g_hbm, r_hbm, l_hbm,
    out_v, gi_v, gr_v, gl_v,
    a_v, g_v, r_v, l_v,
    fo32, fs, fr,
    gf32, gs, gb,
    tl_s, tl_r, tr_s, tr_r,
    in_sem,
    fs_sem, fr_sem, gs_sem, gb_sem,
    ls_sem, lr_sem, rs_sem, rr_sem,
):
    M, D, nb, B, T, rows, scale, NC, H, GROUPS = cfg
    jc, hj = nb // NC, nb // H
    mp, dp = lax.axis_index("mp"), lax.axis_index("dp")

    half = nb // 2
    others = [lax.rem(mp + s, M) for s in range(1, M)]
    early = sum(1 for group in GROUPS if group[0] == 0)
    loads = []
    for src, dst, parts in (
        (a_hbm, a_v, 2), (r_hbm, r_v, 2), (l_hbm, l_v, 1), (g_hbm, g_v, 1)
    ):
        for p in range(parts):
            at = pl.ds(p * (nb // parts), nb // parts)
            loads.append(
                pltpu.make_async_copy(src.at[at], dst.at[at], in_sem.at[len(loads)])
            )
    for n in (0, 2, 1, 3, 4, 5):
        loads[n].start()

    barrier = pltpu.get_barrier_semaphore()
    for s in range(1, M):
        pl.semaphore_signal(
            barrier, inc=1, device_id={"mp": lax.rem(mp + s, M)}, device_id_type=MESH
        )
    for s in range(1, D):
        pl.semaphore_signal(
            barrier, inc=1, device_id={"dp": lax.rem(dp + s, D)}, device_id_type=MESH
        )

    def first(i, carry):
        fo32[pl.ds(i, B, stride=nb), :] = dot(r_v[i], a_v[i], 0, 0)
        return carry

    mine = mp * nb
    forward = [[] for _ in range(NC)]
    def pack_one(dst, j, row, p):
        at = pl.multiple_of(j * nb + p * half, half)
        dst[p, row] = fo32[pl.ds(at, half), :].astype(BF16)

    def send_forward(c, first_part, parts):
        for s, target in enumerate(others, 1):
            base = target * nb + c * jc

            def pack(j, carry, base=base):
                for p in range(first_part, first_part + parts):
                    pack_one(fs, base + j, base + j, p)
                return carry

            lax.fori_loop(0, jc, pack, 0, unroll=4)
            copy = remote(
                fs.at[pl.ds(first_part, parts), pl.ds(base, jc)],
                fr.at[mp, pl.ds(first_part, parts), pl.ds(c * jc, jc)],
                fs_sem.at[c * 2 + first_part, s - 1],
                fr_sem.at[c * 2 + first_part, s - 1],
                "mp",
                target,
            )
            copy.start()
            forward[c].append(copy)

    for p in range(2):
        loads[p].wait()
        loads[2 + p].wait()
        lax.fori_loop(p * half, (p + 1) * half, first, 0, unroll=8)
        if p == 0:
            pl.semaphore_wait(barrier, (M - 1) + (D - 1))
        for c in range(AHEAD):
            send_forward(c, p, 1)

    def own(j, carry):
        for p in range(2):
            pack_one(fr.at[mp], mine + j, j, p)
        return carry

    lax.fori_loop(0, nb, own, 0, unroll=4)
    loads[4].wait()
    loads[5].wait()

    def second(jj, carry):
        x, left = fr[:, :, jj].reshape(B, T), l_v[jj]
        value, slope = gelu_and_slope(dot(left, x, 0, 0))
        out_v[jj] = value.astype(BF16)
        grad_pre = (g_v[jj].astype(F32) * slope).astype(BF16)
        gf32[pl.ds(pl.multiple_of(jj * B, B), B), :] = dot(left, grad_pre, 1, 0)
        term = (dot(x, grad_pre, 1, 1) * scale).astype(BF16)
        for d in range(D):
            tl_s[d, jj] = term[d * rows : (d + 1) * rows]
        return carry

    back, sums_l = [[] for _ in range(len(GROUPS))], []

    def turn(h, start, size, target):
        base = target * nb + start

        def one(i, carry):
            part = gf32[pl.ds(h * hj * B + base + i, hj, stride=B), :]
            gs[h, base + i] = part.astype(BF16)
            return carry

        lax.fori_loop(0, size, one, 0, unroll=8)

    def turn_own(h):
        def one(i, carry):
            part = gf32[pl.ds(h * hj * B + mine + i, hj, stride=B), :]
            gb[mp, h, i] = part.astype(BF16)
            return carry

        lax.fori_loop(0, nb, one, 0, unroll=8)

    def turn_and_send(n):
        h, start, size = GROUPS[n]
        for s, target in enumerate(others, 1):
            turn(h, start, size, target)
            copy = remote(
                gs.at[h, pl.ds(target * nb + start, size)],
                gb.at[mp, h, pl.ds(start, size)],
                gs_sem.at[n, s - 1],
                gb_sem.at[n, s - 1],
                "mp",
                target,
            )
            copy.start()
            back[n].append(copy)

    def send_l(h):
        for s in range(1, D):
            target = lax.rem(dp + s, D)
            copy = remote(
                tl_s.at[target, pl.ds(h * hj, hj)],
                tl_r.at[s - 1, pl.ds(h * hj, hj)],
                ls_sem.at[h, s - 1],
                lr_sem.at[h, s - 1],
                "dp",
                target,
            )
            copy.start()
            sums_l.append(copy)

    for c in range(NC):
        for copy in forward[c]:
            copy.wait_recv()
        if c + AHEAD < NC:
            send_forward(c + AHEAD, 0, 2)
        else:
            turn_and_send(c + AHEAD - NC)
            if c == NC - 1:
                for n in range(AHEAD, early):
                    turn_and_send(n)
        lax.fori_loop(c * jc, (c + 1) * jc, second, 0, unroll=4)
        if c == NC // H - 1:
            send_l(0)
            turn_own(0)
    for n in range(BACK):
        turn_and_send(early + n)
    send_l(1)
    turn_own(1)

    def add_l(jj, carry):
        total = tl_s[dp, jj].astype(F32)
        for s in range(D - 1):
            total = total + tl_r[s, jj].astype(F32)
        gl_v[jj] = total
        return carry

    def last(ii, carry):
        y = gb[:, :, ii].reshape(B, T)
        gi_v[ii] = dot(r_v[ii], y, 1, 0).astype(BF16)
        term = (dot(a_v[ii], y, 1, 1) * scale).astype(BF16)
        for d in range(D):
            tr_s[d, ii] = term[d * rows : (d + 1) * rows]
        return carry

    sums_r = []

    def send_r(g):
        at = pl.ds(*GROUPS[early + g][1:])
        step = []
        for s in range(1, D):
            target = lax.rem(dp + s, D)
            copy = remote(
                tr_s.at[target, at],
                tr_r.at[s - 1, at],
                rs_sem.at[g, s - 1],
                rr_sem.at[g, s - 1],
                "dp",
                target,
            )
            copy.start()
            step.append(copy)
        sums_r.append(step)

    def add_r(ii, carry):
        total = tr_s[dp, ii].astype(F32)
        for s in range(D - 1):
            total = total + tr_r[s, ii].astype(F32)
        gr_v[ii] = total
        return carry

    def finish(g):
        start, size = GROUPS[early + g][1:]
        for copy in sums_r[g]:
            copy.wait_recv()
        lax.fori_loop(start, start + size, add_r, 0, unroll=4)

    count = len(GROUPS) - early
    for g in range(count):
        start, size = GROUPS[early + g][1:]
        for n in range(early):
            if GROUPS[n][1] == start:
                for copy in back[n]:
                    copy.wait_recv()
        for copy in back[early + g]:
            copy.wait_recv()
        if g + BACK < count:
            turn_and_send(early + g + BACK)
        lax.fori_loop(start, start + size, last, 0, unroll=4)
        send_r(g)
        if g == 1:
            for copy in sums_l:
                copy.wait_recv()
            lax.fori_loop(0, nb, add_l, 0, unroll=2)
    for g in range(count):
        finish(g)

    for step in forward + back + sums_r:
        for copy in step:
            copy.wait_send()
    for copy in sums_l:
        copy.wait_send()


def write_out(*refs):
    done = refs[8]
    copies = [pltpu.make_async_copy(refs[n], refs[4 + n], done.at[n]) for n in range(4)]
    for copy in copies:
        copy.start()
    for copy in copies:
        copy.wait()


def fused(M, D, inputs, cotangent, r_factor, l_factor):
    nb, B = r_factor.shape[1], r_factor.shape[2]
    T = inputs.shape[1]
    rows = B // D
    scale = float(D * T) ** (-0.5)
    NC, H = 4, 2
    half, part, small = nb // 2, nb // 4, nb // 8
    groups = ((0, 0, half), (0, half, half))
    groups += ((1, 0, part), (1, part, part), (1, half, part))
    groups += ((1, half + part, small), (1, half + part + small, small))
    cfg = (M, D, nb, B, T, rows, scale, NC, H, groups)
    count = sum(1 for group in groups if group[0] == 1)
    sem = pltpu.SemaphoreType.DMA
    flops = 6 * 2 * nb * B * B * T
    results = pl.pallas_call(
        functools.partial(kernel, cfg),
        out_shape=(
            pltpu.VMEM((nb, B, T), BF16),
            pltpu.VMEM((nb, B, T), BF16),
            pltpu.VMEM((nb, rows, B), F32),
            pltpu.VMEM((nb, rows, B), F32),
        ),
        in_specs=[pl.BlockSpec(memory_space=pltpu.HBM)] * 4,
        out_specs=[pl.BlockSpec(memory_space=pltpu.VMEM)] * 4,
        scratch_shapes=[
            pltpu.VMEM((nb, B, T), BF16),
            pltpu.VMEM((nb, B, T), BF16),
            pltpu.VMEM((nb, B, B), BF16),
            pltpu.VMEM((nb, B, B), BF16),
            pltpu.VMEM((B * nb, T), F32),
            pltpu.VMEM((2, B, half, T), BF16),
            pltpu.VMEM((M, 2, nb, half, T), BF16),
            pltpu.VMEM((nb * B, T), F32),
            pltpu.VMEM((H, B, nb // H, T), BF16),
            pltpu.VMEM((M, H, nb, nb // H, T), BF16),
            pltpu.VMEM((D, nb, rows, B), BF16),
            pltpu.VMEM((D - 1, nb, rows, B), BF16),
            pltpu.VMEM((D, nb, rows, B), BF16),
            pltpu.VMEM((D - 1, nb, rows, B), BF16),
            sem((6,)),
            sem((NC * 2, M - 1)),
            sem((NC * 2, M - 1)),
            sem((len(groups), M - 1)),
            sem((len(groups), M - 1)),
            sem((H, D - 1)),
            sem((H, D - 1)),
            sem((count, D - 1)),
            sem((count, D - 1)),
        ],
        compiler_params=pltpu.CompilerParams(
            collective_id=0, has_side_effects=True, vmem_limit_bytes=61 * 2**20
        ),
        cost_estimate=pl.CostEstimate(
            flops=flops, bytes_accessed=8 * nb * B * T * 2, transcendentals=nb * B * T
        ),
        name="monarch",
    )(
        inputs.reshape(nb, B, T),
        cotangent.reshape(nb, B, T),
        r_factor[0],
        l_factor[0],
    )
    outputs, grad_inputs, grad_r, grad_l = pl.pallas_call(
        write_out,
        out_shape=[jax.ShapeDtypeStruct(x.shape, x.dtype) for x in results],
        in_specs=[pl.BlockSpec(memory_space=pl.ANY)] * 4,
        out_specs=[pl.BlockSpec(memory_space=pltpu.HBM)] * 4,
        scratch_shapes=[sem((4,))],
        compiler_params=pltpu.CompilerParams(vmem_limit_bytes=4 * 2**20),
        name="write_out",
    )(*results)
    return (
        outputs.reshape(nb * B, T),
        grad_inputs.reshape(nb * B, T),
        grad_r[None],
        grad_l[None],
    )


def plain(M, D, inputs, cotangent, r_factor, l_factor):
    nb, B = r_factor.shape[1], r_factor.shape[2]
    T = inputs.shape[1]
    scale = float(D * T) ** (-0.5)
    right, left = r_factor[0], l_factor[0]
    current = inputs.reshape(nb, B, T)
    first_out = jnp.einsum("ikt,ikj->ijt", current, right, preferred_element_type=F32)
    received = lax.all_to_all(
        first_out.astype(BF16), "mp", split_axis=1, concat_axis=0, tiled=True
    )
    pre_act = jnp.einsum("ijt,jim->jmt", received, left, preferred_element_type=F32)
    value, slope = gelu_and_slope(pre_act)
    grad_pre = (cotangent.reshape(nb, B, T).astype(F32) * slope).astype(BF16)
    term_l = jnp.einsum("ijt,jmt->jim", received, grad_pre, preferred_element_type=F32)
    grad_l = lax.psum_scatter(term_l * scale, "dp", scatter_dimension=1, tiled=True)
    grad_first = jnp.einsum("jmt,jim->ijt", grad_pre, left, preferred_element_type=F32)
    returned = lax.all_to_all(
        grad_first.astype(BF16), "mp", split_axis=0, concat_axis=1, tiled=True
    )
    spread = jnp.einsum("ijt,ikj->ikt", returned, right, preferred_element_type=F32)
    term_r = jnp.einsum("ikt,ijt->ikj", current, returned, preferred_element_type=F32)
    grad_r = lax.psum_scatter(term_r * scale, "dp", scatter_dimension=1, tiled=True)
    return (
        value.astype(BF16).reshape(nb * B, T),
        spread.astype(BF16).reshape(nb * B, T),
        grad_r[None],
        grad_l[None],
    )


def solution(mesh):
    M, D = mesh.shape["mp"], mesh.shape["dp"]

    def shards(inputs, cotangent, r_factor, l_factor):
        nb, B = r_factor.shape[1], r_factor.shape[2]
        tiled = nb % 32 == 0 and (B // D) % 16 == 0 and M > 1 and D > 1
        return (fused if tiled else plain)(M, D, inputs, cotangent, r_factor, l_factor)

    return jax.shard_map(
        shards,
        mesh=mesh,
        in_specs=(P("mp", "dp"), P("mp", "dp"), P(None, "mp"), P(None, "mp")),
        out_specs=(P("mp", "dp"), P("mp", "dp"), P(None, "mp", "dp"), P(None, "mp", "dp")),
        check_vma=False,
    )
```

```python
import functools

import jax
import jax.numpy as jnp
from jax import lax
from jax.experimental import pallas as pl
from jax.experimental.pallas import tpu as pltpu
from jax.sharding import PartitionSpec as P

MESH = pl.DeviceIdType.MESH
F32 = jnp.float32
BF16 = jnp.bfloat16
AHEAD = 2
BACK = 2


def dot(left, right, left_dim, right_dim):
    return lax.dot_general(
        left, right, (((left_dim,), (right_dim,)), ((), ())), preferred_element_type=F32
    )


def gelu_and_slope(v):
    c0, c1 = 0.7978845608028654, 0.044715
    square = v * v
    tanh = jnp.tanh(c0 * v * (1.0 + c1 * square))
    half = 0.5 + 0.5 * tanh
    slope = half + 0.5 * v * (1.0 - tanh * tanh) * (c0 + (3.0 * c0 * c1) * square)
    return v * half, slope


def remote(src, dst, send_sem, recv_sem, axis, target):
    return pltpu.make_async_remote_copy(
        src_ref=src,
        dst_ref=dst,
        send_sem=send_sem,
        recv_sem=recv_sem,
        device_id={axis: target},
        device_id_type=MESH,
    )


def kernel(
    cfg,
    a_hbm, g_hbm, r_hbm, l_hbm,
    out_v, gi_v, gr_v, gl_v,
    a_v, g_v, r_v, l_v,
    fo32, fs, fr,
    gf32, gs, gb,
    tl_s, tl_r, tr_s, tr_r,
    in_sem,
    fs_sem, fr_sem, gs_sem, gb_sem,
    ls_sem, lr_sem, rs_sem, rr_sem,
):
    M, D, nb, B, T, rows, scale, NC, H, GROUPS = cfg
    jc, hj = nb // NC, nb // H
    mp, dp = lax.axis_index("mp"), lax.axis_index("dp")

    half = nb // 2
    turns = [1 + lax.rem(n + lax.rem(dp, 2), M - 1) for n in range(M - 1)]
    others = [(s, lax.rem(mp + s, M)) for s in turns]
    early = sum(1 for group in GROUPS if group[0] == 0)
    loads = []
    for src, dst, parts in (
        (a_hbm, a_v, 2), (r_hbm, r_v, 2), (l_hbm, l_v, 1), (g_hbm, g_v, 1)
    ):
        for p in range(parts):
            at = pl.ds(p * (nb // parts), nb // parts)
            loads.append(
                pltpu.make_async_copy(src.at[at], dst.at[at], in_sem.at[len(loads)])
            )
    for n in (0, 2, 1, 3, 4, 5):
        loads[n].start()

    barrier = pltpu.get_barrier_semaphore()
    for s in range(1, M):
        pl.semaphore_signal(
            barrier, inc=1, device_id={"mp": lax.rem(mp + s, M)}, device_id_type=MESH
        )
    for s in range(1, D):
        pl.semaphore_signal(
            barrier, inc=1, device_id={"dp": lax.rem(dp + s, D)}, device_id_type=MESH
        )

    def first(i, carry):
        fo32[pl.ds(i, B, stride=nb), :] = dot(r_v[i], a_v[i], 0, 0)
        return carry

    mine = mp * nb
    forward = [[] for _ in range(NC)]
    def pack_one(dst, j, row, p):
        at = pl.multiple_of(j * nb + p * half, half)
        dst[p, row] = fo32[pl.ds(at, half), :].astype(BF16)

    def send_forward(c, first_part, parts):
        for s, target in others:
            base = target * nb + c * jc

            def pack(j, carry, base=base):
                for p in range(first_part, first_part + parts):
                    pack_one(fs, base + j, base + j, p)
                return carry

            lax.fori_loop(0, jc, pack, 0, unroll=4)
            copy = remote(
                fs.at[pl.ds(first_part, parts), pl.ds(base, jc)],
                fr.at[mp, pl.ds(first_part, parts), pl.ds(c * jc, jc)],
                fs_sem.at[c * 2 + first_part, s - 1],
                fr_sem.at[c * 2 + first_part, s - 1],
                "mp",
                target,
            )
            copy.start()
            forward[c].append(copy)

    for p in range(2):
        loads[p].wait()
        loads[2 + p].wait()
        lax.fori_loop(p * half, (p + 1) * half, first, 0, unroll=8)
        if p == 0:
            pl.semaphore_wait(barrier, (M - 1) + (D - 1))
        for c in range(AHEAD):
            send_forward(c, p, 1)

    def own(j, carry):
        for p in range(2):
            pack_one(fr.at[mp], mine + j, j, p)
        return carry

    lax.fori_loop(0, nb, own, 0, unroll=4)
    loads[4].wait()
    loads[5].wait()

    def second(jj, carry):
        x, left = fr[:, :, jj].reshape(B, T), l_v[jj]
        value, slope = gelu_and_slope(dot(left, x, 0, 0))
        out_v[jj] = value.astype(BF16)
        grad_pre = (g_v[jj].astype(F32) * slope).astype(BF16)
        gf32[pl.ds(pl.multiple_of(jj * B, B), B), :] = dot(left, grad_pre, 1, 0)
        term = (dot(x, grad_pre, 1, 1) * scale).astype(BF16)
        for d in range(D):
            tl_s[d, jj] = term[d * rows : (d + 1) * rows]
        return carry

    back, sums_l = [[] for _ in range(len(GROUPS))], []

    def turn(h, start, size, target):
        base = target * nb + start

        def one(i, carry):
            part = gf32[pl.ds(h * hj * B + base + i, hj, stride=B), :]
            gs[h, base + i] = part.astype(BF16)
            return carry

        lax.fori_loop(0, size, one, 0, unroll=8)

    def turn_own(h):
        def one(i, carry):
            part = gf32[pl.ds(h * hj * B + mine + i, hj, stride=B), :]
            gb[mp, h, i] = part.astype(BF16)
            return carry

        lax.fori_loop(0, nb, one, 0, unroll=8)

    def turn_and_send(n):
        h, start, size = GROUPS[n]
        for s, target in others:
            turn(h, start, size, target)
            copy = remote(
                gs.at[h, pl.ds(target * nb + start, size)],
                gb.at[mp, h, pl.ds(start, size)],
                gs_sem.at[n, s - 1],
                gb_sem.at[n, s - 1],
                "mp",
                target,
            )
            copy.start()
            back[n].append(copy)

    def send_l(h):
        for s in range(1, D):
            target = lax.rem(dp + s, D)
            copy = remote(
                tl_s.at[target, pl.ds(h * hj, hj)],
                tl_r.at[s - 1, pl.ds(h * hj, hj)],
                ls_sem.at[h, s - 1],
                lr_sem.at[h, s - 1],
                "dp",
                target,
            )
            copy.start()
            sums_l.append(copy)

    for c in range(NC):
        for copy in forward[c]:
            copy.wait_recv()
        if c + AHEAD < NC:
            send_forward(c + AHEAD, 0, 2)
        else:
            turn_and_send(c + AHEAD - NC)
            if c == NC - 1:
                for n in range(AHEAD, early):
                    turn_and_send(n)
        lax.fori_loop(c * jc, (c + 1) * jc, second, 0, unroll=4)
        if c == NC // H - 1:
            send_l(0)
            turn_own(0)
    for n in range(BACK):
        turn_and_send(early + n)
    send_l(1)
    turn_own(1)

    def add_l(jj, carry):
        total = tl_s[dp, jj].astype(F32)
        for s in range(D - 1):
            total = total + tl_r[s, jj].astype(F32)
        gl_v[jj] = total
        return carry

    def last(ii, carry):
        y = gb[:, :, ii].reshape(B, T)
        gi_v[ii] = dot(r_v[ii], y, 1, 0).astype(BF16)
        term = (dot(a_v[ii], y, 1, 1) * scale).astype(BF16)
        for d in range(D):
            tr_s[d, ii] = term[d * rows : (d + 1) * rows]
        return carry

    sums_r = []

    def send_r(g):
        at = pl.ds(*GROUPS[early + g][1:])
        step = []
        for s in range(1, D):
            target = lax.rem(dp + s, D)
            copy = remote(
                tr_s.at[target, at],
                tr_r.at[s - 1, at],
                rs_sem.at[g, s - 1],
                rr_sem.at[g, s - 1],
                "dp",
                target,
            )
            copy.start()
            step.append(copy)
        sums_r.append(step)

    def add_r(ii, carry):
        total = tr_s[dp, ii].astype(F32)
        for s in range(D - 1):
            total = total + tr_r[s, ii].astype(F32)
        gr_v[ii] = total
        return carry

    def finish(g):
        start, size = GROUPS[early + g][1:]
        for copy in sums_r[g]:
            copy.wait_recv()
        lax.fori_loop(start, start + size, add_r, 0, unroll=4)

    count = len(GROUPS) - early
    for g in range(count):
        start, size = GROUPS[early + g][1:]
        for n in range(early):
            if GROUPS[n][1] == start:
                for copy in back[n]:
                    copy.wait_recv()
        for copy in back[early + g]:
            copy.wait_recv()
        if g + BACK < count:
            turn_and_send(early + g + BACK)
        lax.fori_loop(start, start + size, last, 0, unroll=4)
        send_r(g)
        if g == 1:
            for copy in sums_l:
                copy.wait_recv()
            lax.fori_loop(0, nb, add_l, 0, unroll=2)
    for g in range(count):
        finish(g)

    for step in forward + back + sums_r:
        for copy in step:
            copy.wait_send()
    for copy in sums_l:
        copy.wait_send()


def write_out(*refs):
    done = refs[8]
    copies = [pltpu.make_async_copy(refs[n], refs[4 + n], done.at[n]) for n in range(4)]
    for copy in copies:
        copy.start()
    for copy in copies:
        copy.wait()


def fused(M, D, inputs, cotangent, r_factor, l_factor):
    nb, B = r_factor.shape[1], r_factor.shape[2]
    T = inputs.shape[1]
    rows = B // D
    scale = float(D * T) ** (-0.5)
    NC, H = 4, 2
    half, part, small = nb // 2, nb // 4, nb // 8
    groups = ((0, 0, half), (0, half, half))
    groups += ((1, 0, part), (1, part, part), (1, half, part))
    groups += ((1, half + part, small), (1, half + part + small, small))
    cfg = (M, D, nb, B, T, rows, scale, NC, H, groups)
    count = sum(1 for group in groups if group[0] == 1)
    sem = pltpu.SemaphoreType.DMA
    flops = 6 * 2 * nb * B * B * T
    results = pl.pallas_call(
        functools.partial(kernel, cfg),
        out_shape=(
            pltpu.VMEM((nb, B, T), BF16),
            pltpu.VMEM((nb, B, T), BF16),
            pltpu.VMEM((nb, rows, B), F32),
            pltpu.VMEM((nb, rows, B), F32),
        ),
        in_specs=[pl.BlockSpec(memory_space=pltpu.HBM)] * 4,
        out_specs=[pl.BlockSpec(memory_space=pltpu.VMEM)] * 4,
        scratch_shapes=[
            pltpu.VMEM((nb, B, T), BF16),
            pltpu.VMEM((nb, B, T), BF16),
            pltpu.VMEM((nb, B, B), BF16),
            pltpu.VMEM((nb, B, B), BF16),
            pltpu.VMEM((B * nb, T), F32),
            pltpu.VMEM((2, B, half, T), BF16),
            pltpu.VMEM((M, 2, nb, half, T), BF16),
            pltpu.VMEM((nb * B, T), F32),
            pltpu.VMEM((H, B, nb // H, T), BF16),
            pltpu.VMEM((M, H, nb, nb // H, T), BF16),
            pltpu.VMEM((D, nb, rows, B), BF16),
            pltpu.VMEM((D - 1, nb, rows, B), BF16),
            pltpu.VMEM((D, nb, rows, B), BF16),
            pltpu.VMEM((D - 1, nb, rows, B), BF16),
            sem((6,)),
            sem((NC * 2, M - 1)),
            sem((NC * 2, M - 1)),
            sem((len(groups), M - 1)),
            sem((len(groups), M - 1)),
            sem((H, D - 1)),
            sem((H, D - 1)),
            sem((count, D - 1)),
            sem((count, D - 1)),
        ],
        compiler_params=pltpu.CompilerParams(
            collective_id=0, has_side_effects=True, vmem_limit_bytes=61 * 2**20
        ),
        cost_estimate=pl.CostEstimate(
            flops=flops, bytes_accessed=8 * nb * B * T * 2, transcendentals=nb * B * T
        ),
        name="monarch",
    )(
        inputs.reshape(nb, B, T),
        cotangent.reshape(nb, B, T),
        r_factor[0],
        l_factor[0],
    )
    outputs, grad_inputs, grad_r, grad_l = pl.pallas_call(
        write_out,
        out_shape=[jax.ShapeDtypeStruct(x.shape, x.dtype) for x in results],
        in_specs=[pl.BlockSpec(memory_space=pl.ANY)] * 4,
        out_specs=[pl.BlockSpec(memory_space=pltpu.HBM)] * 4,
        scratch_shapes=[sem((4,))],
        compiler_params=pltpu.CompilerParams(vmem_limit_bytes=4 * 2**20),
        name="write_out",
    )(*results)
    return (
        outputs.reshape(nb * B, T),
        grad_inputs.reshape(nb * B, T),
        grad_r[None],
        grad_l[None],
    )


def plain(M, D, inputs, cotangent, r_factor, l_factor):
    nb, B = r_factor.shape[1], r_factor.shape[2]
    T = inputs.shape[1]
    scale = float(D * T) ** (-0.5)
    right, left = r_factor[0], l_factor[0]
    current = inputs.reshape(nb, B, T)
    first_out = jnp.einsum("ikt,ikj->ijt", current, right, preferred_element_type=F32)
    received = lax.all_to_all(
        first_out.astype(BF16), "mp", split_axis=1, concat_axis=0, tiled=True
    )
    pre_act = jnp.einsum("ijt,jim->jmt", received, left, preferred_element_type=F32)
    value, slope = gelu_and_slope(pre_act)
    grad_pre = (cotangent.reshape(nb, B, T).astype(F32) * slope).astype(BF16)
    term_l = jnp.einsum("ijt,jmt->jim", received, grad_pre, preferred_element_type=F32)
    grad_l = lax.psum_scatter(term_l * scale, "dp", scatter_dimension=1, tiled=True)
    grad_first = jnp.einsum("jmt,jim->ijt", grad_pre, left, preferred_element_type=F32)
    returned = lax.all_to_all(
        grad_first.astype(BF16), "mp", split_axis=0, concat_axis=1, tiled=True
    )
    spread = jnp.einsum("ijt,ikj->ikt", returned, right, preferred_element_type=F32)
    term_r = jnp.einsum("ikt,ijt->ikj", current, returned, preferred_element_type=F32)
    grad_r = lax.psum_scatter(term_r * scale, "dp", scatter_dimension=1, tiled=True)
    return (
        value.astype(BF16).reshape(nb * B, T),
        spread.astype(BF16).reshape(nb * B, T),
        grad_r[None],
        grad_l[None],
    )


def solution(mesh):
    M, D = mesh.shape["mp"], mesh.shape["dp"]

    def shards(inputs, cotangent, r_factor, l_factor):
        nb, B = r_factor.shape[1], r_factor.shape[2]
        tiled = nb % 32 == 0 and (B // D) % 16 == 0 and M > 2 and D > 1
        return (fused if tiled else plain)(M, D, inputs, cotangent, r_factor, l_factor)

    return jax.shard_map(
        shards,
        mesh=mesh,
        in_specs=(P("mp", "dp"), P("mp", "dp"), P(None, "mp"), P(None, "mp")),
        out_specs=(P("mp", "dp"), P("mp", "dp"), P(None, "mp", "dp"), P(None, "mp", "dp")),
        check_vma=False,
    )
```
